32 devices in a mesh: parts: 2 (over y), blk: 4 (over z), tp: 2 (over x), sub: 2 (over core).
Axes of the slice: x: 2, y: 2, z: 4, core: 2. Of those that a mesh axis runs over, the one named last changes fastest.
Arguments:
- inputs: bfloat16 [2048, 4096], P(('parts', 'blk')), parts along dimension 0, may hold values from -20 to 20
- context_gradient: bfloat16 [2048, 4096], P(('parts', 'blk'), ('tp', 'sub')), parts along dimension 0, may hold values from -6 to 6
- positions: int32 [2048], P(('parts', 'blk')), parts along dimension 0, may hold values from 0 to 255, as said below
- query_weight: bfloat16 [4096, 4096], P('blk', ('tp', 'sub')), may hold values from -0.09375 to 0.09375
- key_value_weight: bfloat16 [4096, 2, 1024], P('blk', 'sub', 'tp'), may hold values from -0.09375 to 0.09375
Outputs:
- grad_inputs: bfloat16 [2048, 4096], P(('parts', 'blk'), ('tp', 'sub')), parts along dimension 0
- grad_query: bfloat16 [8192, 4096], P(('parts', 'blk'), ('tp', 'sub')), parts along dimension 0
- grad_keyval: bfloat16 [8192, 2, 1024], P(('parts', 'blk'), 'sub', 'tp'), parts along dimension 0
The draws below stay inside these ranges and needn't reach their ends.
There are 2 independent parts, one for each index of `parts`. The reference program is written for one: setup_inputs(seed, part) draws one part's arguments, and reference() takes and returns one part's arrays. A program takes and returns all parts, laid end to end along the dimension named above; an argument that names none is the same for every part. Nothing has to cross between parts.
Inputs may be any that keep to these rules, and one draw needn't show every extreme that they name: `positions`: each aligned block of 256 tokens holds whole sequences in order: a position is 0 where a sequence starts and one more than the previous token's otherwise; the first block is one sequence.
All inputs are finite; a program needn't handle non-finite values.
Results may differ from the reference program's by a relative error of at most 0.011.
Values may be sent and summed in bfloat16 or wider, within the bound.
A program may use at most 128 MiB of HBM per device.

```python
import math
import jax
import jax.numpy as jnp
from jax import lax

INPUT_FEATURES = 4096
QUERY_HEADS = 32
KEYVAL_HEADS = 8
HEAD_SIZE = 128
TOKENS_PER_BLOCK = 256
TOKEN_TOTAL = 1024
QUERY_PER_GROUP = 4


def draw_positions(key, part):
    key = jax.random.fold_in(key, 11)
    block_list = TOKEN_TOTAL // TOKENS_PER_BLOCK
    offsets = jnp.arange(TOKENS_PER_BLOCK, dtype=jnp.int32)
    starts_mask = jax.random.randint(key, (block_list, TOKENS_PER_BLOCK), 0, 48) == 0
    starts_mask = starts_mask.at[:, 0].set(True)
    starts_mask = starts_mask.at[0, :].set(offsets == 0)
    starts = lax.cummax(jnp.where(starts_mask, offsets[None, :], 0), axis=1)
    return (offsets[None, :] - starts).reshape(TOKEN_TOTAL).astype(jnp.int32)


def draw_inputs(key, part):
    key = jax.random.fold_in(key, 5)
    first_key = jax.random.fold_in(key, 0)
    normal_part = jax.random.normal(first_key, (TOKEN_TOTAL, INPUT_FEATURES), jnp.float32)
    return jnp.clip(normal_part, -6.0, 6.0).astype(jnp.bfloat16)


def steps_of(key, shape, shards, smallest, high):
    level, own = 1.0, jax.random.fold_in(key, 6)
    for axis_at, shards_of in shards:
        draws = jnp.exp(jax.random.uniform(jax.random.fold_in(own, axis_at), (shards_of,), jnp.float32, smallest / len(shards), high / len(shards)))
        level = level * jnp.repeat(draws, shape[axis_at] // shards_of).reshape([-1 if axis == axis_at else 1 for axis in range(len(shape))])
    return level


def bell_draw(rng, shape, scale, limit, shards=(), held_as=jnp.bfloat16):
    loudness = steps_of(rng, shape, shards, -0.22, 0.18) if shards else 1.0
    entries = jax.random.normal(rng, shape, jnp.float32) * scale * loudness
    return jnp.minimum(jnp.maximum(entries, -limit), limit).astype(held_as)


def setup_inputs(seed: int = 0, part: int = 0) -> dict:
    splits = jax.random.split(jax.random.key(seed), 6)
    own_keys = jax.random.split(jax.random.fold_in(splits[5], part), 6)
    inputs = draw_inputs(jax.random.fold_in(jax.random.fold_in(splits[5], part), 71), part)
    context_gradient = bell_draw(own_keys[1], (TOKEN_TOTAL, QUERY_HEADS * HEAD_SIZE), 1.0, 6.0, ((0, 4), (1, 4)))
    positions = draw_positions(jax.random.fold_in(jax.random.fold_in(splits[5], part), 71), part)
    query_weight = bell_draw(splits[3], (INPUT_FEATURES, QUERY_HEADS * HEAD_SIZE), INPUT_FEATURES ** -0.5, 0.09375, ((0, 4), (1, 4)))
    key_value_weight = bell_draw(splits[4], (INPUT_FEATURES, 2, KEYVAL_HEADS * HEAD_SIZE), INPUT_FEATURES ** -0.5, 0.09375, ((0, 4), (1, 2), (2, 2)))
    return {"inputs": inputs, "context_gradient": context_gradient, "positions": positions, "query_weight": query_weight, "key_value_weight": key_value_weight}


ROPE_BASE = 500000.0

def rotary_tables(positions, head_width):
    half_width = head_width // 2
    frequency = jnp.exp(jnp.arange(half_width, dtype=jnp.float32) * (-2.0 * math.log(ROPE_BASE) / head_width))
    angles = positions.astype(jnp.float32)[:, None] * frequency[None, :]
    cosine_lookup = jnp.concatenate([jnp.cos(angles), jnp.cos(angles)], axis=1)
    sine_lookup = jnp.concatenate([jnp.sin(angles), jnp.sin(angles)], axis=1)
    return (cosine_lookup, sine_lookup)

def rotate(tensor, cosine_lookup, sine_lookup):
    half_width = tensor.shape[-1] // 2
    turned = jnp.concatenate([-tensor[..., half_width:], tensor[..., :half_width]], axis=-1)
    return tensor * cosine_lookup[:, None, :] + turned * sine_lookup[:, None, :]

def inverse_rotation(gradient, cosine_lookup, sine_lookup):
    half_width = gradient.shape[-1] // 2
    shifted = gradient * sine_lookup[:, None, :]
    turned = jnp.concatenate([shifted[..., half_width:], -shifted[..., :half_width]], axis=-1)
    return gradient * cosine_lookup[:, None, :] + turned

def allowed_pairs(positions):
    offsets = jnp.arange(positions.shape[0], dtype=jnp.int32)
    starts = offsets - positions.astype(jnp.int32)
    return (offsets[None, :] <= offsets[:, None]) & (starts[:, None] == starts[None, :])

def attend_back(query_rot, key_rot, value_rows, grad_block, allowed):
    score_scale = 1.0 / math.sqrt(query_rot.shape[-1])
    scores = jnp.einsum('qhd,khd->hqk', query_rot.astype(jnp.float32), key_rot.astype(jnp.float32)) * score_scale
    scores = jnp.where(allowed[None], scores, -jnp.inf)
    row_peak = lax.optimization_barrier(jnp.max(scores, axis=-1, keepdims=True))
    weights = jnp.exp(scores - row_peak)
    probability = weights / lax.optimization_barrier(jnp.sum(weights, axis=-1, keepdims=True))
    prob_rounded = probability.astype(jnp.bfloat16)
    grad_prob = jnp.einsum('qhd,khd->hqk', grad_block.astype(jnp.float32), value_rows.astype(jnp.float32))
    row_delta = lax.optimization_barrier(jnp.sum(probability * grad_prob, axis=-1, keepdims=True))
    grad_score = (probability * (grad_prob - row_delta) * score_scale).astype(jnp.bfloat16)
    grad_query = jnp.einsum('hqk,khd->qhd', grad_score.astype(jnp.float32), key_rot.astype(jnp.float32))
    key_gradient = jnp.einsum('hqk,qhd->khd', grad_score.astype(jnp.float32), query_rot.astype(jnp.float32))
    value_gradient = jnp.einsum('hqk,qhd->khd', prob_rounded.astype(jnp.float32), grad_block.astype(jnp.float32))
    return (grad_query, key_gradient, value_gradient)

def reference(inputs, context_gradient, positions, query_weight, key_value_weight):
    query_complete = jnp.dot(inputs, query_weight, preferred_element_type=jnp.float32).astype(jnp.bfloat16)
    key_complete = jnp.dot(inputs, key_value_weight[:, 0, :], preferred_element_type=jnp.float32).astype(jnp.bfloat16)
    value_complete = jnp.dot(inputs, key_value_weight[:, 1, :], preferred_element_type=jnp.float32).astype(jnp.bfloat16)
    block_list = TOKEN_TOTAL // TOKENS_PER_BLOCK

    def block_function(operands):
        query_block, key_block, value_block, grad_block, position_block = operands
        cosine_lookup, sine_lookup = rotary_tables(position_block, HEAD_SIZE)
        query_rot = rotate(query_block.astype(jnp.float32), cosine_lookup, sine_lookup).astype(jnp.bfloat16)
        key_rot = rotate(key_block.astype(jnp.float32), cosine_lookup, sine_lookup).astype(jnp.bfloat16)
        key_full = jnp.repeat(key_rot, QUERY_PER_GROUP, axis=1)
        value_full = jnp.repeat(value_block, QUERY_PER_GROUP, axis=1)
        grad_query, key_gradient, value_gradient = attend_back(query_rot, key_full, value_full, grad_block, allowed_pairs(position_block))
        query_gradient_rows = inverse_rotation(grad_query, cosine_lookup, sine_lookup).astype(jnp.bfloat16)
        key_gradient_rows = inverse_rotation(key_gradient.reshape(TOKENS_PER_BLOCK, KEYVAL_HEADS, QUERY_PER_GROUP, HEAD_SIZE).sum(axis=2), cosine_lookup, sine_lookup).astype(jnp.bfloat16)
        value_gradient_rows = value_gradient.reshape(TOKENS_PER_BLOCK, KEYVAL_HEADS, QUERY_PER_GROUP, HEAD_SIZE).sum(axis=2).astype(jnp.bfloat16)
        return (query_gradient_rows, key_gradient_rows, value_gradient_rows)
    query_gradient_rows, key_gradient_rows, value_gradient_rows = lax.map(block_function, (query_complete.reshape(block_list, TOKENS_PER_BLOCK, QUERY_HEADS, HEAD_SIZE), key_complete.reshape(block_list, TOKENS_PER_BLOCK, KEYVAL_HEADS, HEAD_SIZE), value_complete.reshape(block_list, TOKENS_PER_BLOCK, KEYVAL_HEADS, HEAD_SIZE), context_gradient.reshape(block_list, TOKENS_PER_BLOCK, QUERY_HEADS, HEAD_SIZE), positions.reshape(block_list, TOKENS_PER_BLOCK)))
    query_gradient_rows = query_gradient_rows.reshape(TOKEN_TOTAL, QUERY_HEADS * HEAD_SIZE)
    key_gradient_rows = key_gradient_rows.reshape(TOKEN_TOTAL, KEYVAL_HEADS * HEAD_SIZE)
    value_gradient_rows = value_gradient_rows.reshape(TOKEN_TOTAL, KEYVAL_HEADS * HEAD_SIZE)
    grad_query = jnp.dot(inputs.T, query_gradient_rows, preferred_element_type=jnp.float32).astype(jnp.bfloat16)
    grad_keys = jnp.dot(inputs.T, key_gradient_rows, preferred_element_type=jnp.float32)
    grad_values = jnp.dot(inputs.T, value_gradient_rows, preferred_element_type=jnp.float32)
    grad_keyval = jnp.stack([grad_keys, grad_values], axis=1).astype(jnp.bfloat16)
    grad_inputs = jnp.dot(query_gradient_rows, query_weight.T, preferred_element_type=jnp.float32)
    grad_inputs = grad_inputs + jnp.dot(key_gradient_rows, key_value_weight[:, 0, :].T, preferred_element_type=jnp.float32)
    grad_inputs = grad_inputs + jnp.dot(value_gradient_rows, key_value_weight[:, 1, :].T, preferred_element_type=jnp.float32)
    return (grad_inputs.astype(jnp.bfloat16), grad_query, grad_keyval)
```

```python
import math

import jax
import jax.numpy as jnp
from jax import lax
from jax.sharding import PartitionSpec as P

HEAD_SIZE = 128
QUERY_PER_GROUP = 4


ROPE_BASE = 500000.0


def from_partner(array, axis, apart):
    return lax.ppermute(array, axis, [(i, i ^ 1 << apart) for i in range(lax.axis_size(axis))])


def passed_along(value, axis, steps):
    count = lax.axis_size(axis)
    pairs = [(source, (source + steps) % count) for source in range(count)]
    return lax.ppermute(value, axis, pairs)


def rotary_tables(positions, head_width):
    half_width = head_width // 2
    frequency = jnp.exp(
        jnp.arange(half_width, dtype=jnp.float32) * (-2.0 * math.log(ROPE_BASE) / head_width)
    )
    angles = positions.astype(jnp.float32)[:, None] * frequency[None, :]
    cosine_lookup = jnp.concatenate([jnp.cos(angles), jnp.cos(angles)], axis=1)
    sine_lookup = jnp.concatenate([jnp.sin(angles), jnp.sin(angles)], axis=1)
    return (cosine_lookup, sine_lookup)


def rotate(tensor, cosine_lookup, sine_lookup):
    half_width = tensor.shape[-1] // 2
    turned = jnp.concatenate([-tensor[..., half_width:], tensor[..., :half_width]], axis=-1)
    return tensor * cosine_lookup[:, None, :] + turned * sine_lookup[:, None, :]


def inverse_rotation(gradient, cosine_lookup, sine_lookup):
    half_width = gradient.shape[-1] // 2
    shifted = gradient * sine_lookup[:, None, :]
    turned = jnp.concatenate([shifted[..., half_width:], -shifted[..., :half_width]], axis=-1)
    return gradient * cosine_lookup[:, None, :] + turned


def allowed_pairs(positions):
    offsets = jnp.arange(positions.shape[0], dtype=jnp.int32)
    starts = offsets - positions
    return (offsets[None, :] <= offsets[:, None]) & (starts[:, None] == starts[None, :])


def attend_back(query_rot, key_rot, value_rows, grad_block, allowed):
    score_scale = 1.0 / math.sqrt(query_rot.shape[-1])
    scores = (
        jnp.einsum("qhd,khd->hqk", query_rot, key_rot, preferred_element_type=jnp.float32)
        * score_scale
    )
    scores = jnp.where(allowed[None], scores, -jnp.inf)
    row_peak = jnp.max(scores, axis=-1, keepdims=True)
    weights = jnp.exp(scores - row_peak)
    probability = weights / jnp.sum(weights, axis=-1, keepdims=True)
    prob_rounded = probability.astype(jnp.bfloat16)
    grad_prob = jnp.einsum(
        "qhd,khd->hqk", grad_block, value_rows, preferred_element_type=jnp.float32
    )
    row_delta = jnp.sum(probability * grad_prob, axis=-1, keepdims=True)
    grad_score = (probability * (grad_prob - row_delta) * score_scale).astype(jnp.bfloat16)
    grad_query = jnp.einsum("hqk,khd->qhd", grad_score, key_rot, preferred_element_type=jnp.float32)
    key_gradient = jnp.einsum(
        "hqk,qhd->khd", grad_score, query_rot, preferred_element_type=jnp.float32
    )
    value_gradient = jnp.einsum(
        "hqk,qhd->khd", prob_rounded, grad_block, preferred_element_type=jnp.float32
    )
    return (grad_query, key_gradient, value_gradient)


def ring_sum(term, axis):
    count = lax.axis_size(axis)
    here = lax.axis_index(axis)
    total = None
    for step in range(count):
        block = term(jnp.mod(here - step - 1, count))
        if total is not None:
            block = block + passed_along(total, axis, 1).astype(jnp.float32)
        total = block.astype(jnp.bfloat16)
    return total


def ring_gather(value, axis):
    count = lax.axis_size(axis)
    here = lax.axis_index(axis)
    whole = jnp.zeros((count,) + value.shape, value.dtype)
    for step in range(count):
        whole = lax.dynamic_update_index_in_dim(whole, value, jnp.mod(here - step, count), 0)
        if step + 1 < count:
            value = passed_along(value, axis, 1)
    return whole


def on_device(inputs, context_gradient, positions, query_weight, key_value_weight):
    tok_rows = inputs.shape[0]
    block_rows = query_weight.shape[0]
    query_cols = query_weight.shape[1]
    local_heads = query_cols // HEAD_SIZE
    local_groups = key_value_weight.shape[2] // HEAD_SIZE
    pair_index = lax.axis_index("sub")
    blocks = lax.axis_size("blk")
    sharers = lax.axis_size("tp") * lax.axis_size("sub")
    share = lax.axis_index("tp") * lax.axis_size("sub") + pair_index
    weight_cols = jnp.concatenate([query_weight, key_value_weight.reshape(block_rows, -1)], axis=1)
    share_rows = tok_rows // sharers
    shared = lax.dynamic_slice_in_dim(inputs, share * share_rows, share_rows, 0)
    shared = lax.all_to_all(
        shared.reshape(share_rows, blocks, block_rows).transpose(1, 0, 2), "blk", 0, 0, tiled=True
    )
    columns = lax.all_gather(shared, ("tp", "sub"), axis=1, tiled=True)

    def projection_term(block):
        rows = lax.dynamic_index_in_dim(columns, block, 0, keepdims=False)
        return jnp.dot(rows, weight_cols, preferred_element_type=jnp.float32)

    projection = ring_sum(projection_term, "blk")
    query_rows = projection[:, :query_cols].reshape(tok_rows, local_heads, HEAD_SIZE)
    own_proj = projection[:, query_cols:]
    peer_proj = from_partner(own_proj, "sub", 0)
    key_rows = jnp.where(pair_index == 0, own_proj, peer_proj).reshape(
        tok_rows, local_groups, HEAD_SIZE
    )
    value_rows = jnp.where(pair_index == 0, peer_proj, own_proj).reshape(
        tok_rows, local_groups, HEAD_SIZE
    )
    cosine_lookup, sine_lookup = rotary_tables(positions, HEAD_SIZE)
    query_rot = rotate(query_rows.astype(jnp.float32), cosine_lookup, sine_lookup).astype(
        jnp.bfloat16
    )
    key_rot = rotate(key_rows.astype(jnp.float32), cosine_lookup, sine_lookup).astype(jnp.bfloat16)
    head_group = (
        pair_index * local_heads + jnp.arange(local_heads, dtype=jnp.int32)
    ) // QUERY_PER_GROUP
    group_pick = (head_group[:, None] == jnp.arange(local_groups, dtype=jnp.int32)[None, :]).astype(
        jnp.bfloat16
    )
    key_full = jnp.einsum(
        "kgd,hg->khd", key_rot, group_pick, preferred_element_type=jnp.float32
    ).astype(jnp.bfloat16)
    value_full = jnp.einsum(
        "kgd,hg->khd", value_rows, group_pick, preferred_element_type=jnp.float32
    ).astype(jnp.bfloat16)
    grad_query, key_gradient, value_gradient = attend_back(
        query_rot,
        key_full,
        value_full,
        context_gradient.reshape(tok_rows, local_heads, HEAD_SIZE),
        allowed_pairs(positions),
    )
    query_gradient_rows = (
        inverse_rotation(grad_query, cosine_lookup, sine_lookup)
        .astype(jnp.bfloat16)
        .reshape(tok_rows, query_cols)
    )
    pick_float = group_pick.astype(jnp.float32)
    key_part = inverse_rotation(
        jnp.einsum("khd,hg->kgd", key_gradient, pick_float, precision=lax.Precision.HIGHEST),
        cosine_lookup,
        sine_lookup,
    )
    value_part = jnp.einsum(
        "khd,hg->kgd", value_gradient, pick_float, precision=lax.Precision.HIGHEST
    )
    mine = jnp.where(pair_index == 0, key_part, value_part)
    other = jnp.where(pair_index == 0, value_part, key_part)
    own_grads = (mine + from_partner(other, "sub", 0)).astype(jnp.bfloat16).reshape(tok_rows, -1)
    grad_proj = jnp.concatenate([query_gradient_rows, own_grads], axis=1)

    all_grads = ring_gather(grad_proj, "blk").reshape(blocks * tok_rows, -1)
    gradient_sum = lax.dot_general(
        columns.reshape(blocks * tok_rows, block_rows),
        all_grads,
        (((0,), (0,)), ((), ())),
        preferred_element_type=jnp.float32,
    ).astype(jnp.bfloat16)
    partial_inputs = lax.dot_general(
        all_grads, weight_cols, (((1,), (1,)), ((), ())), preferred_element_type=jnp.float32
    ).astype(jnp.bfloat16)
    pieces = lax.all_to_all(
        partial_inputs.reshape(sharers, -1, block_rows), ("tp", "sub"), 0, 0, tiled=True
    )
    grad_inputs = jnp.sum(pieces.astype(jnp.float32), axis=0).astype(jnp.bfloat16)
    swaps = [
        (b * sharers + s, s * sharers + b) for b in range(blocks) for s in range(sharers)
    ]
    grad_inputs = lax.ppermute(grad_inputs, ("blk", "tp", "sub"), swaps)
    grad_query_out = gradient_sum[:, :query_cols]
    grad_keyval_out = gradient_sum[:, query_cols:].reshape(block_rows, 1, -1)
    return (grad_inputs, grad_query_out, grad_keyval_out)


def solution(mesh):
    in_specs = (
        P(("parts", "blk"), None),
        P(("parts", "blk"), ("tp", "sub")),
        P(("parts", "blk")),
        P("blk", ("tp", "sub")),
        P("blk", "sub", "tp"),
    )
    out_specs = (
        P(("parts", "blk"), ("tp", "sub")),
        P(("parts", "blk"), ("tp", "sub")),
        P(("parts", "blk"), "sub", "tp"),
    )
    return jax.shard_map(
        on_device, mesh=mesh, in_specs=in_specs, out_specs=out_specs, check_vma=False
    )
```

```python
import math

import jax
import jax.numpy as jnp
from jax import lax
from jax.experimental import pallas as pl
from jax.experimental.pallas import tpu as pltpu
from jax.sharding import PartitionSpec as P

HEAD_SIZE = 128
QUERY_PER_GROUP = 4


ROPE_BASE = 500000.0


def from_partner(array, axis, apart):
    return lax.ppermute(array, axis, [(i, i ^ 1 << apart) for i in range(lax.axis_size(axis))])


def passed_along(value, axis, steps):
    count = lax.axis_size(axis)
    pairs = [(source, (source + steps) % count) for source in range(count)]
    return lax.ppermute(value, axis, pairs)


def rotary_tables(positions, head_width):
    half_width = head_width // 2
    frequency = jnp.exp(
        jnp.arange(half_width, dtype=jnp.float32) * (-2.0 * math.log(ROPE_BASE) / head_width)
    )
    angles = positions.astype(jnp.float32)[:, None] * frequency[None, :]
    cosine_lookup = jnp.concatenate([jnp.cos(angles), jnp.cos(angles)], axis=1)
    sine_lookup = jnp.concatenate([jnp.sin(angles), jnp.sin(angles)], axis=1)
    return (cosine_lookup, sine_lookup)


def rotate(tensor, cosine_lookup, sine_lookup):
    half_width = tensor.shape[-1] // 2
    turned = jnp.concatenate([-tensor[..., half_width:], tensor[..., :half_width]], axis=-1)
    return tensor * cosine_lookup[:, None, :] + turned * sine_lookup[:, None, :]


def inverse_rotation(gradient, cosine_lookup, sine_lookup):
    half_width = gradient.shape[-1] // 2
    shifted = gradient * sine_lookup[:, None, :]
    turned = jnp.concatenate([shifted[..., half_width:], -shifted[..., :half_width]], axis=-1)
    return gradient * cosine_lookup[:, None, :] + turned


def allowed_pairs(positions):
    offsets = jnp.arange(positions.shape[0], dtype=jnp.int32)
    starts = offsets - positions
    return (offsets[None, :] <= offsets[:, None]) & (starts[:, None] == starts[None, :])


def attend_back(query_rot, key_rot, value_rows, grad_block, allowed):
    score_scale = 1.0 / math.sqrt(query_rot.shape[-1])
    scores = (
        jnp.einsum("qhd,khd->hqk", query_rot, key_rot, preferred_element_type=jnp.float32)
        * score_scale
    )
    scores = jnp.where(allowed[None], scores, -jnp.inf)
    row_peak = jnp.max(scores, axis=-1, keepdims=True)
    weights = jnp.exp(scores - row_peak)
    probability = weights / jnp.sum(weights, axis=-1, keepdims=True)
    prob_rounded = probability.astype(jnp.bfloat16)
    grad_prob = jnp.einsum(
        "qhd,khd->hqk", grad_block, value_rows, preferred_element_type=jnp.float32
    )
    row_delta = jnp.sum(probability * grad_prob, axis=-1, keepdims=True)
    grad_score = (probability * (grad_prob - row_delta) * score_scale).astype(jnp.bfloat16)
    grad_query = jnp.einsum("hqk,khd->qhd", grad_score, key_rot, preferred_element_type=jnp.float32)
    key_gradient = jnp.einsum(
        "hqk,qhd->khd", grad_score, query_rot, preferred_element_type=jnp.float32
    )
    value_gradient = jnp.einsum(
        "hqk,qhd->khd", prob_rounded, grad_block, preferred_element_type=jnp.float32
    )
    return (grad_query, key_gradient, value_gradient)


def ring_sum(term, axis):
    count = lax.axis_size(axis)
    here = lax.axis_index(axis)
    total = None
    for step in range(count):
        block = term(jnp.mod(here - step - 1, count))
        if total is not None:
            block = block + passed_along(total, axis, 1).astype(jnp.float32)
        total = block.astype(jnp.bfloat16)
    return total


def ring_gather(value, axis):
    count = lax.axis_size(axis)
    here = lax.axis_index(axis)
    whole = jnp.zeros((count,) + value.shape, value.dtype)
    for step in range(count):
        whole = lax.dynamic_update_index_in_dim(whole, value, jnp.mod(here - step, count), 0)
        if step + 1 < count:
            value = passed_along(value, axis, 1)
    return whole


def fused_kernel(
    x_ref, grad_ref, start_col, start_row, cos_ref, sin_ref, wq_ref, wkv_ref,
    dx_ref, dwq_ref, dwkv_ref,
    w_all, x_all, part, sends, inbox, q_sum, kv_out, kv_in, dkv_out, dkv_in, grads, dx_part,
    dx_send, dx_in, dx_sum, land,
    x_s, x_r, fan_s, fan_r, flow_s, flow_r, kv_s, kv_r, dkv_s, dkv_r, ag_s, ag_r, dx_s, dx_r, end_s, end_r,
):
    size = HEAD_SIZE
    half_q = wq_ref.shape[1] // 2
    width = half_q + 2 * size
    heads = half_q // size
    tokens = x_ref.shape[0]
    depth = wq_ref.shape[0]
    share_rows = tokens // 4
    me = lax.axis_index("blk")
    tp = lax.axis_index("tp")
    sub = lax.axis_index("sub")
    share = tp * 2 + sub
    low = me < 2
    middle = (me == 1) | (me == 2)
    outer = jnp.logical_not(middle)
    order = [jnp.where(low, 3 - j, j) for j in range(4)]
    ahead = jnp.where(low, me + 1, me - 1)
    behind = jnp.where(low, jnp.maximum(me - 1, 0), jnp.minimum(me + 1, 3))
    main = jnp.where(low, 0, 1)
    others = [order[0], order[1], jnp.where(middle, order[3], order[2])]
    mates = [lax.rem(share + r, 4) for r in (1, 2, 3)]

    def send(src, dst, send_sem, recv_sem, **where):
        return pltpu.make_async_remote_copy(
            src_ref=src, dst_ref=dst, send_sem=send_sem, recv_sem=recv_sem,
            device_id=where, device_id_type=pl.DeviceIdType.MESH,
        )

    barrier = pltpu.get_barrier_semaphore()
    for j in others:
        pl.semaphore_signal(barrier, inc=1, device_id={"blk": j}, device_id_type=pl.DeviceIdType.MESH)
    for q in mates:
        pl.semaphore_signal(
            barrier, inc=1, device_id={"tp": q // 2, "sub": lax.rem(q, 2)},
            device_id_type=pl.DeviceIdType.MESH,
        )
    crossing = me != share

    @pl.when(crossing)
    def _():
        pl.semaphore_signal(
            barrier, inc=1,
            device_id={"blk": share, "tp": me // 2, "sub": lax.rem(me, 2)},
            device_id_type=pl.DeviceIdType.MESH,
        )

    pl.semaphore_wait(barrier, 6 + jnp.where(crossing, 1, 0))

    my_rows = pl.ds(pl.multiple_of(share * share_rows, share_rows), share_rows)

    def rows_of(q):
        return pl.ds(pl.multiple_of(q * share_rows, share_rows), share_rows)

    def x_first(j, t):
        return send(
            x_ref.at[my_rows, pl.ds(pl.multiple_of(j * depth, depth), depth)],
            x_all.at[t, my_rows, :], x_s.at[j], x_r.at[t], blk=j,
        )

    for j in others:
        x_first(j, me).start()

    x_all[me] = x_ref[:, pl.ds(pl.multiple_of(me * depth, depth), depth)]
    for h in range(2):
        w_all[h, :, :half_q] = wq_ref[:, h * half_q : (h + 1) * half_q]
        w_all[h, :, half_q : half_q + size] = wkv_ref[:, h * size : (h + 1) * size]
        w_all[h, :, half_q + size :] = wkv_ref[:, (h + 2) * size : (h + 3) * size]

    def fan(t, r, q):
        return send(
            x_all.at[t, my_rows, :], x_all.at[t, my_rows, :], fan_s.at[t, r], fan_r.at[t, r],
            tp=q // 2, sub=lax.rem(q, 2),
        )

    for t in others:
        x_first(t, t).wait_recv()
        for r in range(3):
            fan(t, r, mates[r]).start()

    def fan_wait(t):
        for r in range(3):
            q = lax.rem(share + 3 - r, 4)
            send(
                x_all.at[t, rows_of(q), :], x_all.at[t, rows_of(q), :], fan_s.at[t, r],
                fan_r.at[t, r], tp=q // 2, sub=lax.rem(q, 2),
            ).wait_recv()

    def flow(h, d, way, to):
        return send(sends.at[h, d], inbox.at[h, way, d], flow_s.at[h, d], flow_r.at[h, way, d], blk=to)

    tile = 256

    def project(h, d):
        @pl.loop(0, width // tile)
        def _(n):
            cols = pl.ds(pl.multiple_of(n * tile, tile), tile)
            part[h, d, :, cols] = jnp.dot(
                x_all[d], w_all[h, :, cols], preferred_element_type=jnp.float32
            )

    for h in range(2):
        for j in range(4):
            d = order[j]
            if h == 0:
                @pl.when(d != me)
                def _():
                    fan_wait(d)
            project(h, d)
            if j < 3:
                @pl.when(outer)
                def _():
                    sends[h, d] = part[h, d].astype(jnp.bfloat16)
                    flow(h, d, main, ahead).start()

    def pass_on(h, d, way, to):
        @pl.when(middle)
        def _():
            flow(h, d, way, to).wait_recv()
            sends[h, d] = (part[h, d] + inbox[h, way, d].astype(jnp.float32)).astype(jnp.bfloat16)
            flow(h, d, way, to).start()

    scale = 1.0 / math.sqrt(size)
    cos = cos_ref[...]
    sin = sin_ref[...]

    def turn(u):
        return u * cos + pltpu.roll(u, size // 2, 1) * sin

    def turn_back(u):
        return u * cos - pltpu.roll(u, size // 2, 1) * sin

    def attend(h):
        flow(h, me, 1 - main, ahead).wait_recv()
        total = part[h, me] + inbox[h, 1 - main, me].astype(jnp.float32)
        part[h, me] = total

        @pl.when(middle)
        def _():
            flow(h, me, main, ahead).wait_recv()
            part[h, me] = part[h, me] + inbox[h, main, me].astype(jnp.float32)

        kv = part[h, me, :, half_q:].astype(jnp.bfloat16)
        first, second = kv[:, :size], kv[:, size:]
        is_key = sub == 0
        own = jnp.where(is_key, first, second)
        kv_out[h] = jnp.where(is_key, second, first)
        swap = send(kv_out.at[h], kv_in.at[h], kv_s.at[h], kv_r.at[h], sub=1 - sub)
        swap.start()
        for i in range(heads):
            q_sum[:, i * size : (i + 1) * size] = turn(
                part[h, me, :, i * size : (i + 1) * size].astype(jnp.bfloat16).astype(jnp.float32)
            ).astype(jnp.bfloat16)
        row = lax.broadcasted_iota(jnp.int32, (tokens, tokens), 0)
        col = lax.broadcasted_iota(jnp.int32, (tokens, tokens), 1)
        allowed = (col <= row) & (start_col[...] == start_row[...])
        swap.wait_recv()
        peer = kv_in[h]
        keys = jnp.where(is_key, own, peer)
        values = jnp.where(is_key, peer, own)
        key_rot = turn(keys.astype(jnp.float32)).astype(jnp.bfloat16)
        key_grad = jnp.zeros((tokens, size), jnp.float32)
        value_grad = jnp.zeros((tokens, size), jnp.float32)
        across = (((1,), (1,)), ((), ()))
        down = (((0,), (0,)), ((), ()))
        for i in range(heads):
            cols = slice(i * size, (i + 1) * size)
            query = q_sum[:, cols]
            grad = grad_ref[:, h * half_q + i * size : h * half_q + (i + 1) * size]
            scores = lax.dot_general(query, key_rot, across, preferred_element_type=jnp.float32)
            scores = jnp.where(allowed, scores * scale, -jnp.inf)
            weights = jnp.exp(scores - jnp.max(scores, axis=1, keepdims=True))
            prob = weights / jnp.sum(weights, axis=1, keepdims=True)
            grad_prob = lax.dot_general(grad, values, across, preferred_element_type=jnp.float32)
            delta = jnp.sum(prob * grad_prob, axis=1, keepdims=True)
            grad_score = (prob * (grad_prob - delta) * scale).astype(jnp.bfloat16)
            grads[h, me, :, cols] = turn_back(
                jnp.dot(grad_score, key_rot, preferred_element_type=jnp.float32)
            ).astype(jnp.bfloat16)
            key_grad += lax.dot_general(grad_score, query, down, preferred_element_type=jnp.float32)
            value_grad += lax.dot_general(
                prob.astype(jnp.bfloat16), grad, down, preferred_element_type=jnp.float32
            )
        key_grad = turn_back(key_grad).astype(jnp.bfloat16)
        value_grad = value_grad.astype(jnp.bfloat16)
        own = jnp.where(is_key, key_grad, value_grad)
        dkv_out[h] = jnp.where(is_key, value_grad, key_grad)
        swap = send(dkv_out.at[h], dkv_in.at[h], dkv_s.at[h], dkv_r.at[h], sub=1 - sub)
        swap.start()
        swap.wait_recv()
        peer = dkv_in[h]
        grads[h, me, :, half_q : half_q + size] = jnp.where(is_key, own, peer)
        grads[h, me, :, half_q + size :] = jnp.where(is_key, peer, own)
        spread(h, me, 0, ahead).start()

        @pl.when(middle)
        def _():
            spread(h, me, 1, behind).start()

    def spread(h, t, way, to):
        return send(grads.at[h, t], grads.at[h, t], ag_s.at[h, t, way], ag_r.at[h, t], blk=to)

    def relay(h, t, way, to):
        @pl.when(middle)
        def _():
            spread(h, t, way, to).wait_recv()
            spread(h, t, way, to).start()

    def weight_grad(h):
        @pl.loop(0, depth // tile)
        def _(n):
            cols = pl.ds(pl.multiple_of(n * tile, tile), tile)
            total = lax.dot_general(
                x_all[0, :, cols], grads[h, 0], (((0,), (0,)), ((), ())),
                preferred_element_type=jnp.float32,
            )
            for t in range(1, 4):
                total += lax.dot_general(
                    x_all[t, :, cols], grads[h, t], (((0,), (0,)), ((), ())),
                    preferred_element_type=jnp.float32,
                )
            total = total.astype(jnp.bfloat16)
            dwq_ref[cols, h * half_q : (h + 1) * half_q] = total[:, :half_q]
            dwkv_ref[cols, h * size : (h + 1) * size] = total[:, half_q : half_q + size]
            dwkv_ref[cols, (h + 2) * size : (h + 3) * size] = total[:, half_q + size :]

    def input_term(h, t, cols):
        return lax.dot_general(
            grads[h, t], w_all[h, cols, :], (((1,), (1,)), ((), ())),
            preferred_element_type=jnp.float32,
        )

    def dx_copy(t, q):
        return send(
            dx_send.at[t], dx_in.at[q], dx_s.at[t], dx_r.at[q], tp=t // 2, sub=lax.rem(t, 2)
        )

    def input_block(t):
        @pl.loop(0, depth // tile)
        def _(n):
            cols = pl.ds(pl.multiple_of(n * tile, tile), tile)
            dx_send[t, :, cols] = (dx_part[t, :, cols] + input_term(1, t, cols)).astype(jnp.bfloat16)

        @pl.when(t != share)
        def _():
            dx_copy(t, share).start()

    for j in range(2):
        pass_on(0, order[j], main, ahead)
    pass_on(0, order[3], 1 - main, behind)
    attend(0)
    pass_on(1, order[0], main, ahead)
    relay(0, order[3], 0, ahead)
    pass_on(1, order[1], main, ahead)
    relay(0, order[1], 1, behind)
    pass_on(1, order[3], 1 - main, behind)
    relay(0, order[0], 1, behind)
    attend(1)

    @pl.when(outer)
    def _():
        for j in (2, 1, 0):
            spread(0, order[j], 0, ahead).wait_recv()

    @pl.loop(0, 4)
    def _(t):
        @pl.loop(0, depth // tile)
        def _(n):
            cols = pl.ds(pl.multiple_of(n * tile, tile), tile)
            dx_part[t, :, cols] = input_term(0, t, cols)

    input_block(me)
    weight_grad(0)

    for mid_t, outer_t, way, to in (
        (order[3], order[2], 0, ahead), (order[1], order[1], 1, behind), (order[0], order[0], 1, behind),
    ):
        relay(1, mid_t, way, to)

        @pl.when(outer)
        def _():
            spread(1, outer_t, 0, ahead).wait_recv()

        input_block(jnp.where(middle, mid_t, outer_t))

    total = dx_send[share].astype(jnp.float32)
    for q in mates:
        dx_copy(share, q).wait_recv()
        total += dx_in[q].astype(jnp.float32)
    dx_sum[...] = total.astype(jnp.bfloat16)
    home = send(
        dx_sum, land, end_s, end_r, blk=share, tp=me // 2, sub=lax.rem(me, 2)
    )

    @pl.when(crossing)
    def _():
        home.start()

    weight_grad(1)

    @pl.when(crossing)
    def _():
        home.wait_recv()
        dx_ref[...] = land[...]
        home.wait_send()

    @pl.when(jnp.logical_not(crossing))
    def _():
        dx_ref[...] = dx_sum[...]

    for j in others:
        x_first(j, me).wait_send()
        for r in range(3):
            fan(j, r, mates[r]).wait_send()
    for h in range(2):
        for j in range(2):
            flow(h, order[j], main, ahead).wait_send()

        @pl.when(outer)
        def _():
            flow(h, order[2], main, ahead).wait_send()

        @pl.when(middle)
        def _():
            flow(h, order[3], main, ahead).wait_send()
            spread(h, me, 1, behind).wait_send()
            spread(h, order[3], 0, ahead).wait_send()
            spread(h, order[1], 1, behind).wait_send()
            spread(h, order[0], 1, behind).wait_send()

        spread(h, me, 0, ahead).wait_send()
        send(kv_out.at[h], kv_in.at[h], kv_s.at[h], kv_r.at[h], sub=1 - sub).wait_send()
        send(dkv_out.at[h], dkv_in.at[h], dkv_s.at[h], dkv_r.at[h], sub=1 - sub).wait_send()
    for q in mates:
        dx_copy(q, share).wait_send()


def fused(inputs, context_gradient, positions, query_weight, key_value_weight):
    tokens = inputs.shape[0]
    depth, query_cols = query_weight.shape
    half_q = query_cols // 2
    width = half_q + 2 * HEAD_SIZE
    cosine_lookup, sine_lookup = rotary_tables(positions, HEAD_SIZE)
    sign = jnp.where(jnp.arange(HEAD_SIZE) < HEAD_SIZE // 2, -1.0, 1.0).astype(jnp.float32)
    starts = jnp.arange(tokens, dtype=jnp.int32) - positions
    bf16, f32 = jnp.bfloat16, jnp.float32
    dma = pltpu.SemaphoreType.DMA
    vmem = pl.BlockSpec(memory_space=pltpu.VMEM)
    grad_inputs, grad_query, grad_keyval = pl.pallas_call(
        fused_kernel,
        out_shape=(
            jax.ShapeDtypeStruct((tokens, depth), bf16),
            jax.ShapeDtypeStruct((depth, query_cols), bf16),
            jax.ShapeDtypeStruct((depth, 4 * HEAD_SIZE), bf16),
        ),
        in_specs=[vmem] * 8,
        out_specs=(vmem,) * 3,
        scratch_shapes=[
            pltpu.VMEM((2, depth, width), bf16),
            pltpu.VMEM((4, tokens, depth), bf16),
            pltpu.VMEM((2, 4, tokens, width), f32),
            pltpu.VMEM((2, 4, tokens, width), bf16),
            pltpu.VMEM((2, 2, 4, tokens, width), bf16),
            pltpu.VMEM((tokens, half_q), bf16),
            pltpu.VMEM((2, tokens, HEAD_SIZE), bf16),
            pltpu.VMEM((2, tokens, HEAD_SIZE), bf16),
            pltpu.VMEM((2, tokens, HEAD_SIZE), bf16),
            pltpu.VMEM((2, tokens, HEAD_SIZE), bf16),
            pltpu.VMEM((2, 4, tokens, width), bf16),
            pltpu.VMEM((4, tokens, depth), f32),
            pltpu.VMEM((4, tokens, depth), bf16),
            pltpu.VMEM((4, tokens, depth), bf16),
            pltpu.VMEM((tokens, depth), bf16),
            pltpu.VMEM((tokens, depth), bf16),
            dma((4,)), dma((4,)), dma((4, 3)), dma((4, 3)), dma((2, 4)), dma((2, 2, 4)),
            dma((2,)), dma((2,)), dma((2,)), dma((2,)), dma((2, 4, 2)), dma((2, 4)),
            dma((4,)), dma((4,)), dma, dma,
        ],
        compiler_params=pltpu.CompilerParams(
            collective_id=0, has_side_effects=True, vmem_limit_bytes=60 * 1024 * 1024
        ),
    )(
        inputs, context_gradient, starts[:, None], starts[None, :], cosine_lookup,
        sine_lookup * sign, query_weight, key_value_weight.reshape(depth, -1),
    )
    return (grad_inputs, grad_query, grad_keyval.reshape(depth, 1, -1))


def on_device(inputs, context_gradient, positions, query_weight, key_value_weight):
    tok_rows = inputs.shape[0]
    block_rows = query_weight.shape[0]
    query_cols = query_weight.shape[1]
    local_heads = query_cols // HEAD_SIZE
    local_groups = key_value_weight.shape[2] // HEAD_SIZE
    sizes = tuple(lax.axis_size(axis) for axis in ("blk", "tp", "sub"))
    if sizes == (4, 2, 2) and (local_heads, local_groups) == (2 * QUERY_PER_GROUP, 4):
        return fused(inputs, context_gradient, positions, query_weight, key_value_weight)
    pair_index = lax.axis_index("sub")
    blocks = lax.axis_size("blk")
    sharers = lax.axis_size("tp") * lax.axis_size("sub")
    share = lax.axis_index("tp") * lax.axis_size("sub") + pair_index
    weight_cols = jnp.concatenate([query_weight, key_value_weight.reshape(block_rows, -1)], axis=1)
    share_rows = tok_rows // sharers
    shared = lax.dynamic_slice_in_dim(inputs, share * share_rows, share_rows, 0)
    shared = lax.all_to_all(
        shared.reshape(share_rows, blocks, block_rows).transpose(1, 0, 2), "blk", 0, 0, tiled=True
    )
    columns = lax.all_gather(shared, ("tp", "sub"), axis=1, tiled=True)

    def projection_term(block):
        rows = lax.dynamic_index_in_dim(columns, block, 0, keepdims=False)
        return jnp.dot(rows, weight_cols, preferred_element_type=jnp.float32)

    projection = ring_sum(projection_term, "blk")
    query_rows = projection[:, :query_cols].reshape(tok_rows, local_heads, HEAD_SIZE)
    own_proj = projection[:, query_cols:]
    peer_proj = from_partner(own_proj, "sub", 0)
    key_rows = jnp.where(pair_index == 0, own_proj, peer_proj).reshape(
        tok_rows, local_groups, HEAD_SIZE
    )
    value_rows = jnp.where(pair_index == 0, peer_proj, own_proj).reshape(
        tok_rows, local_groups, HEAD_SIZE
    )
    cosine_lookup, sine_lookup = rotary_tables(positions, HEAD_SIZE)
    query_rot = rotate(query_rows.astype(jnp.float32), cosine_lookup, sine_lookup).astype(
        jnp.bfloat16
    )
    key_rot = rotate(key_rows.astype(jnp.float32), cosine_lookup, sine_lookup).astype(jnp.bfloat16)
    head_group = (
        pair_index * local_heads + jnp.arange(local_heads, dtype=jnp.int32)
    ) // QUERY_PER_GROUP
    group_pick = (head_group[:, None] == jnp.arange(local_groups, dtype=jnp.int32)[None, :]).astype(
        jnp.bfloat16
    )
    key_full = jnp.einsum(
        "kgd,hg->khd", key_rot, group_pick, preferred_element_type=jnp.float32
    ).astype(jnp.bfloat16)
    value_full = jnp.einsum(
        "kgd,hg->khd", value_rows, group_pick, preferred_element_type=jnp.float32
    ).astype(jnp.bfloat16)
    grad_query, key_gradient, value_gradient = attend_back(
        query_rot,
        key_full,
        value_full,
        context_gradient.reshape(tok_rows, local_heads, HEAD_SIZE),
        allowed_pairs(positions),
    )
    query_gradient_rows = (
        inverse_rotation(grad_query, cosine_lookup, sine_lookup)
        .astype(jnp.bfloat16)
        .reshape(tok_rows, query_cols)
    )
    pick_float = group_pick.astype(jnp.float32)
    key_part = inverse_rotation(
        jnp.einsum("khd,hg->kgd", key_gradient, pick_float, precision=lax.Precision.HIGHEST),
        cosine_lookup,
        sine_lookup,
    )
    value_part = jnp.einsum(
        "khd,hg->kgd", value_gradient, pick_float, precision=lax.Precision.HIGHEST
    )
    mine = jnp.where(pair_index == 0, key_part, value_part)
    other = jnp.where(pair_index == 0, value_part, key_part)
    own_grads = (mine + from_partner(other, "sub", 0)).astype(jnp.bfloat16).reshape(tok_rows, -1)
    grad_proj = jnp.concatenate([query_gradient_rows, own_grads], axis=1)

    all_grads = ring_gather(grad_proj, "blk").reshape(blocks * tok_rows, -1)
    gradient_sum = lax.dot_general(
        columns.reshape(blocks * tok_rows, block_rows),
        all_grads,
        (((0,), (0,)), ((), ())),
        preferred_element_type=jnp.float32,
    ).astype(jnp.bfloat16)
    partial_inputs = lax.dot_general(
        all_grads, weight_cols, (((1,), (1,)), ((), ())), preferred_element_type=jnp.float32
    ).astype(jnp.bfloat16)
    pieces = lax.all_to_all(
        partial_inputs.reshape(sharers, -1, block_rows), ("tp", "sub"), 0, 0, tiled=True
    )
    grad_inputs = jnp.sum(pieces.astype(jnp.float32), axis=0).astype(jnp.bfloat16)
    swaps = [
        (b * sharers + s, s * sharers + b) for b in range(blocks) for s in range(sharers)
    ]
    grad_inputs = lax.ppermute(grad_inputs, ("blk", "tp", "sub"), swaps)
    grad_query_out = gradient_sum[:, :query_cols]
    grad_keyval_out = gradient_sum[:, query_cols:].reshape(block_rows, 1, -1)
    return (grad_inputs, grad_query_out, grad_keyval_out)


def solution(mesh):
    in_specs = (
        P(("parts", "blk"), None),
        P(("parts", "blk"), ("tp", "sub")),
        P(("parts", "blk")),
        P("blk", ("tp", "sub")),
        P("blk", "sub", "tp"),
    )
    out_specs = (
        P(("parts", "blk"), ("tp", "sub")),
        P(("parts", "blk"), ("tp", "sub")),
        P(("parts", "blk"), "sub", "tp"),
    )
    return jax.shard_map(
        on_device, mesh=mesh, in_specs=in_specs, out_specs=out_specs, check_vma=False
    )
```

```python
import math

import jax
import jax.numpy as jnp
import numpy as np
from jax import lax
from jax.experimental import pallas as pl
from jax.experimental.pallas import tpu as pltpu
from jax.sharding import PartitionSpec as P

HEAD_SIZE = 128
QUERY_PER_GROUP = 4


ROPE_BASE = 500000.0


def from_partner(array, axis, apart):
    return lax.ppermute(array, axis, [(i, i ^ 1 << apart) for i in range(lax.axis_size(axis))])


def passed_along(value, axis, steps):
    count = lax.axis_size(axis)
    pairs = [(source, (source + steps) % count) for source in range(count)]
    return lax.ppermute(value, axis, pairs)


def rotary_tables(positions, head_width):
    half_width = head_width // 2
    frequency = jnp.exp(
        jnp.arange(half_width, dtype=jnp.float32) * (-2.0 * math.log(ROPE_BASE) / head_width)
    )
    angles = positions.astype(jnp.float32)[:, None] * frequency[None, :]
    cosine_lookup = jnp.concatenate([jnp.cos(angles), jnp.cos(angles)], axis=1)
    sine_lookup = jnp.concatenate([jnp.sin(angles), jnp.sin(angles)], axis=1)
    return (cosine_lookup, sine_lookup)


def rotate(tensor, cosine_lookup, sine_lookup):
    half_width = tensor.shape[-1] // 2
    turned = jnp.concatenate([-tensor[..., half_width:], tensor[..., :half_width]], axis=-1)
    return tensor * cosine_lookup[:, None, :] + turned * sine_lookup[:, None, :]


def inverse_rotation(gradient, cosine_lookup, sine_lookup):
    half_width = gradient.shape[-1] // 2
    shifted = gradient * sine_lookup[:, None, :]
    turned = jnp.concatenate([shifted[..., half_width:], -shifted[..., :half_width]], axis=-1)
    return gradient * cosine_lookup[:, None, :] + turned


def allowed_pairs(positions):
    offsets = jnp.arange(positions.shape[0], dtype=jnp.int32)
    starts = offsets - positions
    return (offsets[None, :] <= offsets[:, None]) & (starts[:, None] == starts[None, :])


def attend_back(query_rot, key_rot, value_rows, grad_block, allowed):
    score_scale = 1.0 / math.sqrt(query_rot.shape[-1])
    scores = (
        jnp.einsum("qhd,khd->hqk", query_rot, key_rot, preferred_element_type=jnp.float32)
        * score_scale
    )
    scores = jnp.where(allowed[None], scores, -jnp.inf)
    row_peak = jnp.max(scores, axis=-1, keepdims=True)
    weights = jnp.exp(scores - row_peak)
    probability = weights / jnp.sum(weights, axis=-1, keepdims=True)
    prob_rounded = probability.astype(jnp.bfloat16)
    grad_prob = jnp.einsum(
        "qhd,khd->hqk", grad_block, value_rows, preferred_element_type=jnp.float32
    )
    row_delta = jnp.sum(probability * grad_prob, axis=-1, keepdims=True)
    grad_score = (probability * (grad_prob - row_delta) * score_scale).astype(jnp.bfloat16)
    grad_query = jnp.einsum("hqk,khd->qhd", grad_score, key_rot, preferred_element_type=jnp.float32)
    key_gradient = jnp.einsum(
        "hqk,qhd->khd", grad_score, query_rot, preferred_element_type=jnp.float32
    )
    value_gradient = jnp.einsum(
        "hqk,qhd->khd", prob_rounded, grad_block, preferred_element_type=jnp.float32
    )
    return (grad_query, key_gradient, value_gradient)


def ring_sum(term, axis):
    count = lax.axis_size(axis)
    here = lax.axis_index(axis)
    total = None
    for step in range(count):
        block = term(jnp.mod(here - step - 1, count))
        if total is not None:
            block = block + passed_along(total, axis, 1).astype(jnp.float32)
        total = block.astype(jnp.bfloat16)
    return total


def ring_gather(value, axis):
    count = lax.axis_size(axis)
    here = lax.axis_index(axis)
    whole = jnp.zeros((count,) + value.shape, value.dtype)
    for step in range(count):
        whole = lax.dynamic_update_index_in_dim(whole, value, jnp.mod(here - step, count), 0)
        if step + 1 < count:
            value = passed_along(value, axis, 1)
    return whole


def fused_kernel(
    x_ref, grad_hbm, pos_ref, freq_ref, sign_ref, wq_ref, wkv_ref,
    dx_ref, dwq_ref, dwkv_ref,
    w_all, x_all, part, sends, inbox, q_sum, kv_out, kv_in, dkv_out, dkv_in, grads, dx_part,
    pair_send, pair_in, own_sum, side_send, side_in, land, cos_ref, sin_ref, grad_ref, load_s,
    x_s, x_r, fan_s, fan_r, flow_s, flow_r, kv_s, kv_r, dkv_s, dkv_r, ag_s, ag_r, dx_s, dx_r, end_s, end_r, pair_s, pair_r,
):
    size = HEAD_SIZE
    half_q = wq_ref.shape[1] // 2
    width = half_q + 2 * size
    heads = half_q // size
    tokens = x_ref.shape[0]
    depth = wq_ref.shape[0]
    share_rows = tokens // 4
    me = lax.axis_index("blk")
    tp = lax.axis_index("tp")
    sub = lax.axis_index("sub")
    share = tp * 2 + sub
    low = me < 2
    middle = (me == 1) | (me == 2)
    outer = jnp.logical_not(middle)
    order = [jnp.where(low, 3 - j, j) for j in range(4)]
    ahead = jnp.where(low, me + 1, me - 1)
    behind = jnp.where(low, jnp.maximum(me - 1, 0), jnp.minimum(me + 1, 3))
    main = jnp.where(low, 0, 1)
    others = [order[0], order[1], jnp.where(middle, order[3], order[2])]
    mates = [lax.rem(share + r, 4) for r in (1, 2, 3)]

    def send(src, dst, send_sem, recv_sem, **where):
        return pltpu.make_async_remote_copy(
            src_ref=src, dst_ref=dst, send_sem=send_sem, recv_sem=recv_sem,
            device_id=where, device_id_type=pl.DeviceIdType.MESH,
        )

    def apart(blk, x, core):
        same_line = (x == tp) & (core == sub)
        return jnp.logical_not(same_line | (blk == me))

    barrier = pltpu.get_barrier_semaphore()
    for j in others:
        pl.semaphore_signal(barrier, inc=1, device_id={"blk": j}, device_id_type=pl.DeviceIdType.MESH)
    for q in mates:
        pl.semaphore_signal(
            barrier, inc=1, device_id={"tp": q // 2, "sub": lax.rem(q, 2)},
            device_id_type=pl.DeviceIdType.MESH,
        )
    def greet(where, needed):
        @pl.when(needed)
        def _():
            pl.semaphore_signal(barrier, inc=1, device_id=where, device_id_type=pl.DeviceIdType.MESH)

    expected = 6
    for i in range(2):
        target = 2 * tp + i
        needed = apart(target, me // 2, lax.rem(me, 2))
        expected += jnp.where(needed, 1, 0)
        greet({"blk": share, "tp": me // 2, "sub": i}, apart(share, me // 2, i))
    pl.semaphore_wait(barrier, expected)

    my_rows = pl.ds(pl.multiple_of(share * share_rows, share_rows), share_rows)

    def rows_of(q):
        return pl.ds(pl.multiple_of(q * share_rows, share_rows), share_rows)

    def x_first(j, t):
        return send(
            x_ref.at[my_rows, pl.ds(pl.multiple_of(j * depth, depth), depth)],
            x_all.at[t, my_rows, :], x_s.at[j], x_r.at[t], blk=j,
        )

    for j in others:
        x_first(j, me).start()

    loads = [
        (x_ref.at[:, pl.ds(pl.multiple_of(me * depth, depth), depth)], x_all.at[me]),
        (grad_hbm, grad_ref),
    ]
    for h in range(2):
        loads += [
            (wq_ref.at[:, h * half_q : (h + 1) * half_q], w_all.at[h, :, :half_q]),
            (wkv_ref.at[:, h * size : (h + 1) * size], w_all.at[h, :, half_q : half_q + size]),
            (wkv_ref.at[:, (h + 2) * size : (h + 3) * size], w_all.at[h, :, half_q + size :]),
        ]
    loads = [pltpu.make_async_copy(a, b, load_s.at[i]) for i, (a, b) in enumerate(loads)]
    for load in loads:
        load.start()

    places = jnp.broadcast_to(pos_ref[...].astype(jnp.float32), (size, tokens)).T
    angles = places * freq_ref[...]
    cos_ref[...] = jnp.cos(angles)
    sin_ref[...] = jnp.sin(angles) * sign_ref[...]

    def fan(t, r, q):
        return send(
            x_all.at[t, my_rows, :], x_all.at[t, my_rows, :], fan_s.at[t, r], fan_r.at[t, r],
            tp=q // 2, sub=lax.rem(q, 2),
        )

    for t in others:
        x_first(t, t).wait_recv()
        for r in range(3):
            fan(t, r, mates[r]).start()

    for load in loads:
        load.wait()

    def fan_wait(t):
        for r in range(3):
            q = lax.rem(share + 3 - r, 4)
            send(
                x_all.at[t, rows_of(q), :], x_all.at[t, rows_of(q), :], fan_s.at[t, r],
                fan_r.at[t, r], tp=q // 2, sub=lax.rem(q, 2),
            ).wait_recv()

    def flow(h, d, way, to):
        return send(sends.at[h, d], inbox.at[h, way, d], flow_s.at[h, d], flow_r.at[h, way, d], blk=to)

    tile = 256

    def project(h, d):
        @pl.loop(0, width // tile)
        def _(n):
            cols = pl.ds(pl.multiple_of(n * tile, tile), tile)
            part[h, d, :, cols] = jnp.dot(
                x_all[d], w_all[h, :, cols], preferred_element_type=jnp.float32
            )

    def emit(h, j):
        sends[h, order[j]] = part[h, order[j]].astype(jnp.bfloat16)
        if h + j > 0:
            flow(0 if j == 0 else h, order[(j + 2) % 3], main, ahead).wait_send()
        flow(h, order[j], main, ahead).start()

    for h in range(2):
        for j in range(4):
            d = order[j]
            if h == 0:
                @pl.when(d != me)
                def _():
                    fan_wait(d)
            project(h, d)
            if h == 0 and j < 3:
                @pl.when(outer)
                def _():
                    emit(0, j)

    @pl.when(outer)
    def _():
        emit(1, 0)

    def pass_on(h, d, way, to):
        @pl.when(middle)
        def _():
            flow(h, d, way, to).wait_recv()
            sends[h, d] = (part[h, d] + inbox[h, way, d].astype(jnp.float32)).astype(jnp.bfloat16)
            flow(h, d, way, to).start()

    scale = 1.0 / math.sqrt(size)
    cos = cos_ref[...]
    sin = sin_ref[...]

    def turn(u):
        return u * cos + pltpu.roll(u, size // 2, 1) * sin

    def turn_back(u):
        return u * cos - pltpu.roll(u, size // 2, 1) * sin

    def attend(h):
        flow(h, me, 1 - main, ahead).wait_recv()
        total = part[h, me] + inbox[h, 1 - main, me].astype(jnp.float32)
        part[h, me] = total

        @pl.when(middle)
        def _():
            flow(h, me, main, ahead).wait_recv()
            part[h, me] = part[h, me] + inbox[h, main, me].astype(jnp.float32)

        kv = part[h, me, :, half_q:].astype(jnp.bfloat16)
        first, second = kv[:, :size], kv[:, size:]
        is_key = sub == 0
        own = jnp.where(is_key, first, second)
        kv_out[h] = jnp.where(is_key, second, first)
        swap = send(kv_out.at[h], kv_in.at[h], kv_s.at[h], kv_r.at[h], sub=1 - sub)
        swap.start()
        for i in range(heads):
            q_sum[:, i * size : (i + 1) * size] = turn(
                part[h, me, :, i * size : (i + 1) * size].astype(jnp.bfloat16).astype(jnp.float32)
            ).astype(jnp.bfloat16)
        row = lax.broadcasted_iota(jnp.int32, (tokens, tokens), 0)
        col = lax.broadcasted_iota(jnp.int32, (tokens, tokens), 1)
        starts = (col - pos_ref[...]).astype(jnp.float32)
        allowed = (col <= row) & (starts == starts.T)
        swap.wait_recv()
        peer = kv_in[h]
        keys = jnp.where(is_key, own, peer)
        values = jnp.where(is_key, peer, own)
        key_rot = turn(keys.astype(jnp.float32)).astype(jnp.bfloat16)
        key_grad = jnp.zeros((tokens, size), jnp.float32)
        value_grad = jnp.zeros((tokens, size), jnp.float32)
        across = (((1,), (1,)), ((), ()))
        down = (((0,), (0,)), ((), ()))
        for i in range(heads):
            cols = slice(i * size, (i + 1) * size)
            query = q_sum[:, cols]
            grad = grad_ref[:, h * half_q + i * size : h * half_q + (i + 1) * size]
            scores = lax.dot_general(query, key_rot, across, preferred_element_type=jnp.float32)
            scores = jnp.where(allowed, scores * scale, -jnp.inf)
            weights = jnp.exp(scores - jnp.max(scores, axis=1, keepdims=True))
            prob = weights / jnp.sum(weights, axis=1, keepdims=True)
            grad_prob = lax.dot_general(grad, values, across, preferred_element_type=jnp.float32)
            delta = jnp.sum(prob * grad_prob, axis=1, keepdims=True)
            grad_score = (prob * (grad_prob - delta) * scale).astype(jnp.bfloat16)
            grads[h, me, :, cols] = turn_back(
                jnp.dot(grad_score, key_rot, preferred_element_type=jnp.float32)
            ).astype(jnp.bfloat16)
            key_grad += lax.dot_general(grad_score, query, down, preferred_element_type=jnp.float32)
            value_grad += lax.dot_general(
                prob.astype(jnp.bfloat16), grad, down, preferred_element_type=jnp.float32
            )
        key_grad = turn_back(key_grad).astype(jnp.bfloat16)
        value_grad = value_grad.astype(jnp.bfloat16)
        own = jnp.where(is_key, key_grad, value_grad)
        dkv_out[h] = jnp.where(is_key, value_grad, key_grad)
        swap = send(dkv_out.at[h], dkv_in.at[h], dkv_s.at[h], dkv_r.at[h], sub=1 - sub)
        swap.start()
        swap.wait_recv()
        peer = dkv_in[h]
        grads[h, me, :, half_q : half_q + size] = jnp.where(is_key, own, peer)
        grads[h, me, :, half_q + size :] = jnp.where(is_key, peer, own)
        spread(h, me, 0, ahead).start()

        @pl.when(middle)
        def _():
            spread(h, me, 1, behind).start()

    def spread(h, t, way, to):
        return send(grads.at[h, t], grads.at[h, t], ag_s.at[h, t, way], ag_r.at[h, t], blk=to)

    def relay(h, t, way, to):
        @pl.when(middle)
        def _():
            spread(h, t, way, to).wait_recv()
            spread(h, t, way, to).start()

    def weight_grad(h):
        @pl.loop(0, depth // tile)
        def _(n):
            cols = pl.ds(pl.multiple_of(n * tile, tile), tile)
            total = lax.dot_general(
                x_all[0, :, cols], grads[h, 0], (((0,), (0,)), ((), ())),
                preferred_element_type=jnp.float32,
            )
            for t in range(1, 4):
                total += lax.dot_general(
                    x_all[t, :, cols], grads[h, t], (((0,), (0,)), ((), ())),
                    preferred_element_type=jnp.float32,
                )
            total = total.astype(jnp.bfloat16)
            dwq_ref[cols, h * half_q : (h + 1) * half_q] = total[:, :half_q]
            dwkv_ref[cols, h * size : (h + 1) * size] = total[:, half_q : half_q + size]
            dwkv_ref[cols, (h + 2) * size : (h + 3) * size] = total[:, half_q + size :]

    def input_term(h, t, cols):
        return lax.dot_general(
            grads[h, t], w_all[h, cols, :], (((1,), (1,)), ((), ())),
            preferred_element_type=jnp.float32,
        )

    half_d = depth // 2
    mine = pl.ds(pl.multiple_of(sub * half_d, half_d), half_d)
    theirs = pl.ds(pl.multiple_of((1 - sub) * half_d, half_d), half_d)
    home_x, home_sub = me // 2, lax.rem(me, 2)

    def pair_copy(t):
        return send(pair_send.at[t], pair_in.at[t], pair_s.at[t], pair_r.at[t], sub=1 - sub)

    def side_copy(t):
        return send(side_send.at[t], side_in.at[t], dx_s.at[t], dx_r.at[t], tp=1 - tp)

    def home_copy(t, i, where_t):
        return send(
            side_send.at[t], land.at[:, pl.ds(pl.multiple_of(i * half_d, half_d), half_d)],
            end_s.at[t], end_r.at[i], blk=where_t, tp=home_x, sub=home_sub,
        )

    def stays(t):
        return (t == me) & (sub == home_sub)

    def finish(t):
        @pl.when(t // 2 == tp)
        def _():
            side_copy(t).wait_recv()
            side_send[t] = (own_sum[t] + side_in[t].astype(jnp.float32)).astype(jnp.bfloat16)

            @pl.when(stays(t))
            def _():
                land[:, mine] = side_send[t]

            @pl.when(jnp.logical_not(stays(t)))
            def _():
                home_copy(t, sub, t).start()

    def input_block(t):
        @pl.loop(0, half_d // tile)
        def _(n):
            there = pl.ds(pl.multiple_of((1 - sub) * half_d + n * tile, tile), tile)
            cols = pl.ds(pl.multiple_of(n * tile, tile), tile)
            pair_send[t, :, cols] = (dx_part[t, :, there] + input_term(1, t, there)).astype(
                jnp.bfloat16
            )

        pair_copy(t).start()

        @pl.loop(0, half_d // tile)
        def _(n):
            here = pl.ds(pl.multiple_of(sub * half_d + n * tile, tile), tile)
            cols = pl.ds(pl.multiple_of(n * tile, tile), tile)
            own_sum[t, :, cols] = dx_part[t, :, here] + input_term(1, t, here)

        pair_copy(t).wait_recv()
        own_sum[t] = own_sum[t] + pair_in[t].astype(jnp.float32)

        @pl.when(t // 2 != tp)
        def _():
            side_send[t] = own_sum[t].astype(jnp.bfloat16)
            side_copy(t).start()

    for j in range(2):
        pass_on(0, order[j], main, ahead)
    pass_on(0, order[3], 1 - main, behind)
    attend(0)

    @pl.when(outer)
    def _():
        emit(1, 1)
        emit(1, 2)

    pass_on(1, order[0], main, ahead)
    relay(0, order[3], 0, ahead)
    pass_on(1, order[1], main, ahead)
    relay(0, order[1], 1, behind)
    pass_on(1, order[3], 1 - main, behind)
    relay(0, order[0], 1, behind)
    attend(1)

    @pl.when(outer)
    def _():
        for j in (2, 1, 0):
            spread(0, order[j], 0, ahead).wait_recv()

    @pl.loop(0, 4)
    def _(t):
        @pl.loop(0, depth // tile)
        def _(n):
            cols = pl.ds(pl.multiple_of(n * tile, tile), tile)
            dx_part[t, :, cols] = input_term(0, t, cols)

    input_block(me)
    weight_grad(0)
    previous = me

    for mid_t, outer_t, way, to in (
        (order[3], order[2], 0, ahead), (order[1], order[1], 1, behind), (order[0], order[0], 1, behind),
    ):
        relay(1, mid_t, way, to)

        @pl.when(outer)
        def _():
            spread(1, outer_t, 0, ahead).wait_recv()

        latest = jnp.where(middle, mid_t, outer_t)
        input_block(latest)
        finish(previous)
        previous = latest

    finish(previous)
    weight_grad(1)

    for i in range(2):
        @pl.when(jnp.logical_not((share == me) & (sub == i)))
        def _():
            home_copy(me, i, me).wait_recv()

    dx_ref[...] = land[...]
    for t in range(4):
        pair_copy(t).wait_send()

        @pl.when(t // 2 != tp)
        def _():
            side_copy(t).wait_send()

        @pl.when((t // 2 == tp) & jnp.logical_not(stays(t)))
        def _():
            home_copy(t, sub, t).wait_send()

    for j in others:
        x_first(j, me).wait_send()
        for r in range(3):
            fan(j, r, mates[r]).wait_send()
    for h in range(2):
        if h == 1:
            @pl.when(outer)
            def _():
                flow(h, order[2], main, ahead).wait_send()

        @pl.when(middle)
        def _():
            for j in range(2):
                flow(h, order[j], main, ahead).wait_send()
            flow(h, order[3], main, ahead).wait_send()
            spread(h, me, 1, behind).wait_send()
            spread(h, order[3], 0, ahead).wait_send()
            spread(h, order[1], 1, behind).wait_send()
            spread(h, order[0], 1, behind).wait_send()

        spread(h, me, 0, ahead).wait_send()
        send(kv_out.at[h], kv_in.at[h], kv_s.at[h], kv_r.at[h], sub=1 - sub).wait_send()
        send(dkv_out.at[h], dkv_in.at[h], dkv_s.at[h], dkv_r.at[h], sub=1 - sub).wait_send()


def fused(inputs, context_gradient, positions, query_weight, key_value_weight):
    tokens = inputs.shape[0]
    depth, query_cols = query_weight.shape
    half_q = query_cols // 2
    width = half_q + 2 * HEAD_SIZE
    half = np.arange(HEAD_SIZE // 2, dtype=np.float64)
    frequency = np.exp(half * (-2.0 * math.log(ROPE_BASE) / HEAD_SIZE)).astype(np.float32)
    frequency = np.concatenate([frequency, frequency])[None, :]
    sign = np.where(np.arange(HEAD_SIZE) < HEAD_SIZE // 2, -1.0, 1.0).astype(np.float32)[None, :]
    bf16, f32 = jnp.bfloat16, jnp.float32
    dma = pltpu.SemaphoreType.DMA
    vmem = pl.BlockSpec(memory_space=pltpu.VMEM)
    whole = pl.BlockSpec(memory_space=pl.ANY)
    grad_inputs, grad_query, grad_keyval = pl.pallas_call(
        fused_kernel,
        out_shape=(
            jax.ShapeDtypeStruct((tokens, depth), bf16),
            jax.ShapeDtypeStruct((depth, query_cols), bf16),
            jax.ShapeDtypeStruct((depth, 4 * HEAD_SIZE), bf16),
        ),
        in_specs=[whole, whole] + [vmem] * 3 + [whole, whole],
        out_specs=(vmem,) * 3,
        scratch_shapes=[
            pltpu.VMEM((2, depth, width), bf16),
            pltpu.VMEM((4, tokens, depth), bf16),
            pltpu.VMEM((2, 4, tokens, width), f32),
            pltpu.VMEM((2, 4, tokens, width), bf16),
            pltpu.VMEM((2, 2, 4, tokens, width), bf16),
            pltpu.VMEM((tokens, half_q), bf16),
            pltpu.VMEM((2, tokens, HEAD_SIZE), bf16),
            pltpu.VMEM((2, tokens, HEAD_SIZE), bf16),
            pltpu.VMEM((2, tokens, HEAD_SIZE), bf16),
            pltpu.VMEM((2, tokens, HEAD_SIZE), bf16),
            pltpu.VMEM((2, 4, tokens, width), bf16),
            pltpu.VMEM((4, tokens, depth), f32),
            pltpu.VMEM((4, tokens, depth // 2), bf16),
            pltpu.VMEM((4, tokens, depth // 2), bf16),
            pltpu.VMEM((4, tokens, depth // 2), f32),
            pltpu.VMEM((4, tokens, depth // 2), bf16),
            pltpu.VMEM((4, tokens, depth // 2), bf16),
            pltpu.VMEM((tokens, depth), bf16),
            pltpu.VMEM((tokens, HEAD_SIZE), f32),
            pltpu.VMEM((tokens, HEAD_SIZE), f32),
            pltpu.VMEM((tokens, query_cols), bf16),
            dma((8,)),
            dma((4,)), dma((4,)), dma((4, 3)), dma((4, 3)), dma((2, 4)), dma((2, 2, 4)),
            dma((2,)), dma((2,)), dma((2,)), dma((2,)), dma((2, 4, 2)), dma((2, 4)),
            dma((4,)), dma((4,)), dma((4,)), dma((2,)), dma((4,)), dma((4,)),
        ],
        compiler_params=pltpu.CompilerParams(
            collective_id=0, has_side_effects=True, vmem_limit_bytes=60 * 1024 * 1024
        ),
    )(
        inputs, context_gradient, positions[None, :], frequency, sign, query_weight, key_value_weight.reshape(depth, -1),
    )
    return (grad_inputs, grad_query, grad_keyval.reshape(depth, 1, -1))


def on_device(inputs, context_gradient, positions, query_weight, key_value_weight):
    tok_rows = inputs.shape[0]
    block_rows = query_weight.shape[0]
    query_cols = query_weight.shape[1]
    local_heads = query_cols // HEAD_SIZE
    local_groups = key_value_weight.shape[2] // HEAD_SIZE
    sizes = tuple(lax.axis_size(axis) for axis in ("blk", "tp", "sub"))
    if sizes == (4, 2, 2) and (local_heads, local_groups) == (2 * QUERY_PER_GROUP, 4):
        return fused(inputs, context_gradient, positions, query_weight, key_value_weight)
    pair_index = lax.axis_index("sub")
    blocks = lax.axis_size("blk")
    sharers = lax.axis_size("tp") * lax.axis_size("sub")
    share = lax.axis_index("tp") * lax.axis_size("sub") + pair_index
    weight_cols = jnp.concatenate([query_weight, key_value_weight.reshape(block_rows, -1)], axis=1)
    share_rows = tok_rows // sharers
    shared = lax.dynamic_slice_in_dim(inputs, share * share_rows, share_rows, 0)
    shared = lax.all_to_all(
        shared.reshape(share_rows, blocks, block_rows).transpose(1, 0, 2), "blk", 0, 0, tiled=True
    )
    columns = lax.all_gather(shared, ("tp", "sub"), axis=1, tiled=True)

    def projection_term(block):
        rows = lax.dynamic_index_in_dim(columns, block, 0, keepdims=False)
        return jnp.dot(rows, weight_cols, preferred_element_type=jnp.float32)

    projection = ring_sum(projection_term, "blk")
    query_rows = projection[:, :query_cols].reshape(tok_rows, local_heads, HEAD_SIZE)
    own_proj = projection[:, query_cols:]
    peer_proj = from_partner(own_proj, "sub", 0)
    key_rows = jnp.where(pair_index == 0, own_proj, peer_proj).reshape(
        tok_rows, local_groups, HEAD_SIZE
    )
    value_rows = jnp.where(pair_index == 0, peer_proj, own_proj).reshape(
        tok_rows, local_groups, HEAD_SIZE
    )
    cosine_lookup, sine_lookup = rotary_tables(positions, HEAD_SIZE)
    query_rot = rotate(query_rows.astype(jnp.float32), cosine_lookup, sine_lookup).astype(
        jnp.bfloat16
    )
    key_rot = rotate(key_rows.astype(jnp.float32), cosine_lookup, sine_lookup).astype(jnp.bfloat16)
    head_group = (
        pair_index * local_heads + jnp.arange(local_heads, dtype=jnp.int32)
    ) // QUERY_PER_GROUP
    group_pick = (head_group[:, None] == jnp.arange(local_groups, dtype=jnp.int32)[None, :]).astype(
        jnp.bfloat16
    )
    key_full = jnp.einsum(
        "kgd,hg->khd", key_rot, group_pick, preferred_element_type=jnp.float32
    ).astype(jnp.bfloat16)
    value_full = jnp.einsum(
        "kgd,hg->khd", value_rows, group_pick, preferred_element_type=jnp.float32
    ).astype(jnp.bfloat16)
    grad_query, key_gradient, value_gradient = attend_back(
        query_rot,
        key_full,
        value_full,
        context_gradient.reshape(tok_rows, local_heads, HEAD_SIZE),
        allowed_pairs(positions),
    )
    query_gradient_rows = (
        inverse_rotation(grad_query, cosine_lookup, sine_lookup)
        .astype(jnp.bfloat16)
        .reshape(tok_rows, query_cols)
    )
    pick_float = group_pick.astype(jnp.float32)
    key_part = inverse_rotation(
        jnp.einsum("khd,hg->kgd", key_gradient, pick_float, precision=lax.Precision.HIGHEST),
        cosine_lookup,
        sine_lookup,
    )
    value_part = jnp.einsum(
        "khd,hg->kgd", value_gradient, pick_float, precision=lax.Precision.HIGHEST
    )
    mine = jnp.where(pair_index == 0, key_part, value_part)
    other = jnp.where(pair_index == 0, value_part, key_part)
    own_grads = (mine + from_partner(other, "sub", 0)).astype(jnp.bfloat16).reshape(tok_rows, -1)
    grad_proj = jnp.concatenate([query_gradient_rows, own_grads], axis=1)

    all_grads = ring_gather(grad_proj, "blk").reshape(blocks * tok_rows, -1)
    gradient_sum = lax.dot_general(
        columns.reshape(blocks * tok_rows, block_rows),
        all_grads,
        (((0,), (0,)), ((), ())),
        preferred_element_type=jnp.float32,
    ).astype(jnp.bfloat16)
    partial_inputs = lax.dot_general(
        all_grads, weight_cols, (((1,), (1,)), ((), ())), preferred_element_type=jnp.float32
    ).astype(jnp.bfloat16)
    pieces = lax.all_to_all(
        partial_inputs.reshape(sharers, -1, block_rows), ("tp", "sub"), 0, 0, tiled=True
    )
    grad_inputs = jnp.sum(pieces.astype(jnp.float32), axis=0).astype(jnp.bfloat16)
    swaps = [
        (b * sharers + s, s * sharers + b) for b in range(blocks) for s in range(sharers)
    ]
    grad_inputs = lax.ppermute(grad_inputs, ("blk", "tp", "sub"), swaps)
    grad_query_out = gradient_sum[:, :query_cols]
    grad_keyval_out = gradient_sum[:, query_cols:].reshape(block_rows, 1, -1)
    return (grad_inputs, grad_query_out, grad_keyval_out)


def solution(mesh):
    in_specs = (
        P(("parts", "blk"), None),
        P(("parts", "blk"), ("tp", "sub")),
        P(("parts", "blk")),
        P("blk", ("tp", "sub")),
        P("blk", "sub", "tp"),
    )
    out_specs = (
        P(("parts", "blk"), ("tp", "sub")),
        P(("parts", "blk"), ("tp", "sub")),
        P(("parts", "blk"), "sub", "tp"),
    )
    return jax.shard_map(
        on_device, mesh=mesh, in_specs=in_specs, out_specs=out_specs, check_vma=False
    )
```

```python
import math

import jax
import jax.numpy as jnp
import numpy as np
from jax import lax
from jax.experimental import pallas as pl
from jax.experimental.pallas import tpu as pltpu
from jax.sharding import PartitionSpec as P

HEAD_SIZE = 128
QUERY_PER_GROUP = 4


ROPE_BASE = 500000.0


def from_partner(array, axis, apart):
    return lax.ppermute(array, axis, [(i, i ^ 1 << apart) for i in range(lax.axis_size(axis))])


def passed_along(value, axis, steps):
    count = lax.axis_size(axis)
    pairs = [(source, (source + steps) % count) for source in range(count)]
    return lax.ppermute(value, axis, pairs)


def rotary_tables(positions, head_width):
    half_width = head_width // 2
    frequency = jnp.exp(
        jnp.arange(half_width, dtype=jnp.float32) * (-2.0 * math.log(ROPE_BASE) / head_width)
    )
    angles = positions.astype(jnp.float32)[:, None] * frequency[None, :]
    cosine_lookup = jnp.concatenate([jnp.cos(angles), jnp.cos(angles)], axis=1)
    sine_lookup = jnp.concatenate([jnp.sin(angles), jnp.sin(angles)], axis=1)
    return (cosine_lookup, sine_lookup)


def rotate(tensor, cosine_lookup, sine_lookup):
    half_width = tensor.shape[-1] // 2
    turned = jnp.concatenate([-tensor[..., half_width:], tensor[..., :half_width]], axis=-1)
    return tensor * cosine_lookup[:, None, :] + turned * sine_lookup[:, None, :]


def inverse_rotation(gradient, cosine_lookup, sine_lookup):
    half_width = gradient.shape[-1] // 2
    shifted = gradient * sine_lookup[:, None, :]
    turned = jnp.concatenate([shifted[..., half_width:], -shifted[..., :half_width]], axis=-1)
    return gradient * cosine_lookup[:, None, :] + turned


def allowed_pairs(positions):
    offsets = jnp.arange(positions.shape[0], dtype=jnp.int32)
    starts = offsets - positions
    return (offsets[None, :] <= offsets[:, None]) & (starts[:, None] == starts[None, :])


def attend_back(query_rot, key_rot, value_rows, grad_block, allowed):
    score_scale = 1.0 / math.sqrt(query_rot.shape[-1])
    scores = (
        jnp.einsum("qhd,khd->hqk", query_rot, key_rot, preferred_element_type=jnp.float32)
        * score_scale
    )
    scores = jnp.where(allowed[None], scores, -jnp.inf)
    row_peak = jnp.max(scores, axis=-1, keepdims=True)
    weights = jnp.exp(scores - row_peak)
    probability = weights / jnp.sum(weights, axis=-1, keepdims=True)
    prob_rounded = probability.astype(jnp.bfloat16)
    grad_prob = jnp.einsum(
        "qhd,khd->hqk", grad_block, value_rows, preferred_element_type=jnp.float32
    )
    row_delta = jnp.sum(probability * grad_prob, axis=-1, keepdims=True)
    grad_score = (probability * (grad_prob - row_delta) * score_scale).astype(jnp.bfloat16)
    grad_query = jnp.einsum("hqk,khd->qhd", grad_score, key_rot, preferred_element_type=jnp.float32)
    key_gradient = jnp.einsum(
        "hqk,qhd->khd", grad_score, query_rot, preferred_element_type=jnp.float32
    )
    value_gradient = jnp.einsum(
        "hqk,qhd->khd", prob_rounded, grad_block, preferred_element_type=jnp.float32
    )
    return (grad_query, key_gradient, value_gradient)


def ring_sum(term, axis):
    count = lax.axis_size(axis)
    here = lax.axis_index(axis)
    total = None
    for step in range(count):
        block = term(jnp.mod(here - step - 1, count))
        if total is not None:
            block = block + passed_along(total, axis, 1).astype(jnp.float32)
        total = block.astype(jnp.bfloat16)
    return total


def ring_gather(value, axis):
    count = lax.axis_size(axis)
    here = lax.axis_index(axis)
    whole = jnp.zeros((count,) + value.shape, value.dtype)
    for step in range(count):
        whole = lax.dynamic_update_index_in_dim(whole, value, jnp.mod(here - step, count), 0)
        if step + 1 < count:
            value = passed_along(value, axis, 1)
    return whole


def fused_kernel(
    x_ref, grad_hbm, pos_ref, freq_ref, sign_ref, wq_ref, wkv_ref,
    dx_ref, dwq_ref, dwkv_ref,
    w_all, x_all, part, sends, inbox, q_sum, kv_out, kv_in, dkv_out, dkv_in, grads, dx_part,
    pair_send, pair_in, own_sum, side_send, side_in, land, cos_ref, sin_ref, grad_ref, load_s,
    x_s, x_r, fan_s, fan_r, flow_s, flow_r, kv_s, kv_r, dkv_s, dkv_r, ag_s, ag_r, dx_s, dx_r, end_s, end_r, pair_s, pair_r,
):
    size = HEAD_SIZE
    half_q = wq_ref.shape[1] // 2
    width = half_q + 2 * size
    heads = half_q // size
    tokens = x_ref.shape[0]
    depth = wq_ref.shape[0]
    share_rows = tokens // 4
    me = lax.axis_index("blk")
    tp = lax.axis_index("tp")
    sub = lax.axis_index("sub")
    share = tp * 2 + sub
    low = me < 2
    middle = (me == 1) | (me == 2)
    outer = jnp.logical_not(middle)
    order = [jnp.where(low, 3 - j, j) for j in range(4)]
    ahead = jnp.where(low, me + 1, me - 1)
    behind = jnp.where(low, jnp.maximum(me - 1, 0), jnp.minimum(me + 1, 3))
    main = jnp.where(low, 0, 1)
    others = [order[0], order[1], jnp.where(middle, order[3], order[2])]
    mates = [lax.rem(share + r, 4) for r in (1, 2, 3)]

    def send(src, dst, send_sem, recv_sem, **where):
        return pltpu.make_async_remote_copy(
            src_ref=src, dst_ref=dst, send_sem=send_sem, recv_sem=recv_sem,
            device_id=where, device_id_type=pl.DeviceIdType.MESH,
        )

    def apart(blk, x, core):
        same_line = (x == tp) & (core == sub)
        return jnp.logical_not(same_line | (blk == me))

    barrier = pltpu.get_barrier_semaphore()
    for j in others:
        pl.semaphore_signal(barrier, inc=1, device_id={"blk": j}, device_id_type=pl.DeviceIdType.MESH)
    for q in mates:
        pl.semaphore_signal(
            barrier, inc=1, device_id={"tp": q // 2, "sub": lax.rem(q, 2)},
            device_id_type=pl.DeviceIdType.MESH,
        )
    def greet(where, needed):
        @pl.when(needed)
        def _():
            pl.semaphore_signal(barrier, inc=1, device_id=where, device_id_type=pl.DeviceIdType.MESH)

    expected = 6
    for i in range(2):
        target = 2 * tp + i
        needed = apart(target, me // 2, lax.rem(me, 2))
        expected += jnp.where(needed, 1, 0)
        greet({"blk": share, "tp": me // 2, "sub": i}, apart(share, me // 2, i))
    pl.semaphore_wait(barrier, expected)

    my_rows = pl.ds(pl.multiple_of(share * share_rows, share_rows), share_rows)

    def rows_of(q):
        return pl.ds(pl.multiple_of(q * share_rows, share_rows), share_rows)

    def x_first(j, t):
        return send(
            x_ref.at[my_rows, pl.ds(pl.multiple_of(j * depth, depth), depth)],
            x_all.at[t, my_rows, :], x_s.at[j], x_r.at[t], blk=j,
        )

    for j in others:
        x_first(j, me).start()

    loads = [
        (x_ref.at[:, pl.ds(pl.multiple_of(me * depth, depth), depth)], x_all.at[me]),
        (grad_hbm, grad_ref),
    ]
    for h in range(2):
        loads += [
            (wq_ref.at[:, h * half_q : (h + 1) * half_q], w_all.at[h, :, :half_q]),
            (wkv_ref.at[:, h * size : (h + 1) * size], w_all.at[h, :, half_q : half_q + size]),
            (wkv_ref.at[:, (h + 2) * size : (h + 3) * size], w_all.at[h, :, half_q + size :]),
        ]
    loads = [pltpu.make_async_copy(a, b, load_s.at[i]) for i, (a, b) in enumerate(loads)]
    for load in loads:
        load.start()

    places = jnp.broadcast_to(pos_ref[...].astype(jnp.float32), (size, tokens)).T
    angles = places * freq_ref[...]
    cos_ref[...] = jnp.cos(angles)
    sin_ref[...] = jnp.sin(angles) * sign_ref[...]

    def fan(t, kind, row_tp, row_sub):
        rows = rows_of(row_tp * 2 + row_sub)
        where = {"tp": 1 - tp} if kind == 1 else {"sub": 1 - sub}
        return send(
            x_all.at[t, rows, :], x_all.at[t, rows, :], fan_s.at[t, kind], fan_r.at[t, kind], **where
        )

    def fan_own(t):
        x_first(t, t).wait_recv()
        fan(t, 1, tp, sub).start()
        fan(t, 0, tp, sub).start()

    def fan_side(t):
        fan(t, 1, 1 - tp, sub).wait_recv()
        fan(t, 2, 1 - tp, sub).start()

    for load in loads:
        load.wait()

    def fan_wait(t):
        fan(t, 0, tp, 1 - sub).wait_recv()
        fan(t, 2, 1 - tp, 1 - sub).wait_recv()

    def flow(h, d, way, to):
        return send(sends.at[h, d], inbox.at[h, way, d], flow_s.at[h, d], flow_r.at[h, way, d], blk=to)

    tile = 256

    def project(h, d):
        @pl.loop(0, width // tile)
        def _(n):
            cols = pl.ds(pl.multiple_of(n * tile, tile), tile)
            part[h, d, :, cols] = jnp.dot(
                x_all[d], w_all[h, :, cols], preferred_element_type=jnp.float32
            )

    def emit(h, j):
        sends[h, order[j]] = part[h, order[j]].astype(jnp.bfloat16)
        if h + j > 0:
            flow(0 if j == 0 else h, order[(j + 2) % 3], main, ahead).wait_send()
        flow(h, order[j], main, ahead).start()

    for h in range(2):
        for j in range(4):
            d = order[j]
            if h == 0:
                if j == 0:
                    fan_own(others[0])
                    fan_own(others[1])
                    fan_side(others[0])
                elif j == 1:
                    fan_own(others[2])
                    fan_side(others[1])
                elif j == 2:
                    fan_side(others[2])

                @pl.when(d != me)
                def _():
                    fan_wait(d)
            project(h, d)
            if h == 0 and j < 3:
                @pl.when(outer)
                def _():
                    emit(0, j)

    @pl.when(outer)
    def _():
        emit(1, 0)

    def pass_on(h, d, way, to):
        @pl.when(middle)
        def _():
            flow(h, d, way, to).wait_recv()
            sends[h, d] = (part[h, d] + inbox[h, way, d].astype(jnp.float32)).astype(jnp.bfloat16)
            flow(h, d, way, to).start()

    scale = 1.0 / math.sqrt(size)
    cos = cos_ref[...]
    sin = sin_ref[...]

    def turn(u):
        return u * cos + pltpu.roll(u, size // 2, 1) * sin

    def turn_back(u):
        return u * cos - pltpu.roll(u, size // 2, 1) * sin

    def attend(h):
        flow(h, me, 1 - main, ahead).wait_recv()
        total = part[h, me] + inbox[h, 1 - main, me].astype(jnp.float32)
        part[h, me] = total

        @pl.when(middle)
        def _():
            flow(h, me, main, ahead).wait_recv()
            part[h, me] = part[h, me] + inbox[h, main, me].astype(jnp.float32)

        kv = part[h, me, :, half_q:].astype(jnp.bfloat16)
        first, second = kv[:, :size], kv[:, size:]
        is_key = sub == 0
        own = jnp.where(is_key, first, second)
        kv_out[h] = jnp.where(is_key, second, first)
        swap = send(kv_out.at[h], kv_in.at[h], kv_s.at[h], kv_r.at[h], sub=1 - sub)
        swap.start()
        for i in range(heads):
            q_sum[:, i * size : (i + 1) * size] = turn(
                part[h, me, :, i * size : (i + 1) * size].astype(jnp.bfloat16).astype(jnp.float32)
            ).astype(jnp.bfloat16)
        row = lax.broadcasted_iota(jnp.int32, (tokens, tokens), 0)
        col = lax.broadcasted_iota(jnp.int32, (tokens, tokens), 1)
        starts = (col - pos_ref[...]).astype(jnp.float32)
        allowed = (col <= row) & (starts == starts.T)
        swap.wait_recv()
        peer = kv_in[h]
        keys = jnp.where(is_key, own, peer)
        values = jnp.where(is_key, peer, own)
        key_rot = turn(keys.astype(jnp.float32)).astype(jnp.bfloat16)
        key_grad = jnp.zeros((tokens, size), jnp.float32)
        value_grad = jnp.zeros((tokens, size), jnp.float32)
        across = (((1,), (1,)), ((), ()))
        down = (((0,), (0,)), ((), ()))
        for i in range(heads):
            cols = slice(i * size, (i + 1) * size)
            query = q_sum[:, cols]
            grad = grad_ref[:, h * half_q + i * size : h * half_q + (i + 1) * size]
            scores = lax.dot_general(query, key_rot, across, preferred_element_type=jnp.float32)
            scores = jnp.where(allowed, scores * scale, -jnp.inf)
            weights = jnp.exp(scores - jnp.max(scores, axis=1, keepdims=True))
            prob = weights / jnp.sum(weights, axis=1, keepdims=True)
            grad_prob = lax.dot_general(grad, values, across, preferred_element_type=jnp.float32)
            delta = jnp.sum(prob * grad_prob, axis=1, keepdims=True)
            grad_score = (prob * (grad_prob - delta) * scale).astype(jnp.bfloat16)
            grads[h, me, :, cols] = turn_back(
                jnp.dot(grad_score, key_rot, preferred_element_type=jnp.float32)
            ).astype(jnp.bfloat16)
            key_grad += lax.dot_general(grad_score, query, down, preferred_element_type=jnp.float32)
            value_grad += lax.dot_general(
                prob.astype(jnp.bfloat16), grad, down, preferred_element_type=jnp.float32
            )
        key_grad = turn_back(key_grad).astype(jnp.bfloat16)
        value_grad = value_grad.astype(jnp.bfloat16)
        own = jnp.where(is_key, key_grad, value_grad)
        dkv_out[h] = jnp.where(is_key, value_grad, key_grad)
        swap = send(dkv_out.at[h], dkv_in.at[h], dkv_s.at[h], dkv_r.at[h], sub=1 - sub)
        swap.start()
        swap.wait_recv()
        peer = dkv_in[h]
        grads[h, me, :, half_q : half_q + size] = jnp.where(is_key, own, peer)
        grads[h, me, :, half_q + size :] = jnp.where(is_key, peer, own)
        spread(h, me, 0, ahead).start()

        @pl.when(middle)
        def _():
            spread(h, me, 1, behind).start()

    def spread(h, t, way, to):
        return send(grads.at[h, t], grads.at[h, t], ag_s.at[h, t, way], ag_r.at[h, t], blk=to)

    def relay(h, t, way, to):
        @pl.when(middle)
        def _():
            spread(h, t, way, to).wait_recv()
            spread(h, t, way, to).start()

    def weight_grad(h):
        @pl.loop(0, depth // tile)
        def _(n):
            cols = pl.ds(pl.multiple_of(n * tile, tile), tile)
            total = lax.dot_general(
                x_all[0, :, cols], grads[h, 0], (((0,), (0,)), ((), ())),
                preferred_element_type=jnp.float32,
            )
            for t in range(1, 4):
                total += lax.dot_general(
                    x_all[t, :, cols], grads[h, t], (((0,), (0,)), ((), ())),
                    preferred_element_type=jnp.float32,
                )
            total = total.astype(jnp.bfloat16)
            dwq_ref[cols, h * half_q : (h + 1) * half_q] = total[:, :half_q]
            dwkv_ref[cols, h * size : (h + 1) * size] = total[:, half_q : half_q + size]
            dwkv_ref[cols, (h + 2) * size : (h + 3) * size] = total[:, half_q + size :]

    def input_term(h, t, cols):
        return lax.dot_general(
            grads[h, t], w_all[h, cols, :], (((1,), (1,)), ((), ())),
            preferred_element_type=jnp.float32,
        )

    half_d = depth // 2
    mine = pl.ds(pl.multiple_of(sub * half_d, half_d), half_d)
    theirs = pl.ds(pl.multiple_of((1 - sub) * half_d, half_d), half_d)
    home_x, home_sub = me // 2, lax.rem(me, 2)

    def pair_copy(t):
        return send(pair_send.at[t], pair_in.at[t], pair_s.at[t], pair_r.at[t], sub=1 - sub)

    def side_copy(t):
        return send(side_send.at[t], side_in.at[t], dx_s.at[t], dx_r.at[t], tp=1 - tp)

    def home_copy(t, i, where_t):
        return send(
            side_send.at[t], land.at[:, pl.ds(pl.multiple_of(i * half_d, half_d), half_d)],
            end_s.at[t], end_r.at[i], blk=where_t, tp=home_x, sub=home_sub,
        )

    def stays(t):
        return (t == me) & (sub == home_sub)

    def finish(t):
        @pl.when(t // 2 == tp)
        def _():
            side_copy(t).wait_recv()
            side_send[t] = (own_sum[t] + side_in[t].astype(jnp.float32)).astype(jnp.bfloat16)

            @pl.when(stays(t))
            def _():
                land[:, mine] = side_send[t]

            @pl.when(jnp.logical_not(stays(t)))
            def _():
                home_copy(t, sub, t).start()

    def input_block(t):
        @pl.loop(0, half_d // tile)
        def _(n):
            there = pl.ds(pl.multiple_of((1 - sub) * half_d + n * tile, tile), tile)
            cols = pl.ds(pl.multiple_of(n * tile, tile), tile)
            pair_send[t, :, cols] = (dx_part[t, :, there] + input_term(1, t, there)).astype(
                jnp.bfloat16
            )

        pair_copy(t).start()

        @pl.loop(0, half_d // tile)
        def _(n):
            here = pl.ds(pl.multiple_of(sub * half_d + n * tile, tile), tile)
            cols = pl.ds(pl.multiple_of(n * tile, tile), tile)
            own_sum[t, :, cols] = dx_part[t, :, here] + input_term(1, t, here)

        pair_copy(t).wait_recv()
        own_sum[t] = own_sum[t] + pair_in[t].astype(jnp.float32)

        @pl.when(t // 2 != tp)
        def _():
            side_send[t] = own_sum[t].astype(jnp.bfloat16)
            side_copy(t).start()

    for j in range(2):
        pass_on(0, order[j], main, ahead)
    pass_on(0, order[3], 1 - main, behind)
    attend(0)

    @pl.when(outer)
    def _():
        emit(1, 1)
        emit(1, 2)

    pass_on(1, order[0], main, ahead)
    relay(0, order[3], 0, ahead)
    pass_on(1, order[1], main, ahead)
    relay(0, order[1], 1, behind)
    pass_on(1, order[3], 1 - main, behind)
    relay(0, order[0], 1, behind)
    attend(1)

    @pl.when(outer)
    def _():
        for j in (2, 1, 0):
            spread(0, order[j], 0, ahead).wait_recv()

    @pl.loop(0, 4)
    def _(t):
        @pl.loop(0, depth // tile)
        def _(n):
            cols = pl.ds(pl.multiple_of(n * tile, tile), tile)
            dx_part[t, :, cols] = input_term(0, t, cols)

    input_block(me)
    weight_grad(0)
    previous = me

    for mid_t, outer_t, way, to in (
        (order[3], order[2], 0, ahead), (order[1], order[1], 1, behind), (order[0], order[0], 1, behind),
    ):
        relay(1, mid_t, way, to)

        @pl.when(outer)
        def _():
            spread(1, outer_t, 0, ahead).wait_recv()

        latest = jnp.where(middle, mid_t, outer_t)
        input_block(latest)
        finish(previous)
        previous = latest

    finish(previous)
    weight_grad(1)

    for i in range(2):
        @pl.when(jnp.logical_not((share == me) & (sub == i)))
        def _():
            home_copy(me, i, me).wait_recv()

    dx_ref[...] = land[...]
    for t in range(4):
        pair_copy(t).wait_send()

        @pl.when(t // 2 != tp)
        def _():
            side_copy(t).wait_send()

        @pl.when((t // 2 == tp) & jnp.logical_not(stays(t)))
        def _():
            home_copy(t, sub, t).wait_send()

    for j in others:
        x_first(j, me).wait_send()
        fan(j, 0, tp, sub).wait_send()
        fan(j, 1, tp, sub).wait_send()
        fan(j, 2, 1 - tp, sub).wait_send()
    for h in range(2):
        if h == 1:
            @pl.when(outer)
            def _():
                flow(h, order[2], main, ahead).wait_send()

        @pl.when(middle)
        def _():
            for j in range(2):
                flow(h, order[j], main, ahead).wait_send()
            flow(h, order[3], main, ahead).wait_send()
            spread(h, me, 1, behind).wait_send()
            spread(h, order[3], 0, ahead).wait_send()
            spread(h, order[1], 1, behind).wait_send()
            spread(h, order[0], 1, behind).wait_send()

        spread(h, me, 0, ahead).wait_send()
        send(kv_out.at[h], kv_in.at[h], kv_s.at[h], kv_r.at[h], sub=1 - sub).wait_send()
        send(dkv_out.at[h], dkv_in.at[h], dkv_s.at[h], dkv_r.at[h], sub=1 - sub).wait_send()


def fused(inputs, context_gradient, positions, query_weight, key_value_weight):
    tokens = inputs.shape[0]
    depth, query_cols = query_weight.shape
    half_q = query_cols // 2
    width = half_q + 2 * HEAD_SIZE
    half = np.arange(HEAD_SIZE // 2, dtype=np.float64)
    frequency = np.exp(half * (-2.0 * math.log(ROPE_BASE) / HEAD_SIZE)).astype(np.float32)
    frequency = np.concatenate([frequency, frequency])[None, :]
    sign = np.where(np.arange(HEAD_SIZE) < HEAD_SIZE // 2, -1.0, 1.0).astype(np.float32)[None, :]
    bf16, f32 = jnp.bfloat16, jnp.float32
    dma = pltpu.SemaphoreType.DMA
    vmem = pl.BlockSpec(memory_space=pltpu.VMEM)
    whole = pl.BlockSpec(memory_space=pl.ANY)
    grad_inputs, grad_query, grad_keyval = pl.pallas_call(
        fused_kernel,
        out_shape=(
            jax.ShapeDtypeStruct((tokens, depth), bf16),
            jax.ShapeDtypeStruct((depth, query_cols), bf16),
            jax.ShapeDtypeStruct((depth, 4 * HEAD_SIZE), bf16),
        ),
        in_specs=[whole, whole] + [vmem] * 3 + [whole, whole],
        out_specs=(vmem,) * 3,
        scratch_shapes=[
            pltpu.VMEM((2, depth, width), bf16),
            pltpu.VMEM((4, tokens, depth), bf16),
            pltpu.VMEM((2, 4, tokens, width), f32),
            pltpu.VMEM((2, 4, tokens, width), bf16),
            pltpu.VMEM((2, 2, 4, tokens, width), bf16),
            pltpu.VMEM((tokens, half_q), bf16),
            pltpu.VMEM((2, tokens, HEAD_SIZE), bf16),
            pltpu.VMEM((2, tokens, HEAD_SIZE), bf16),
            pltpu.VMEM((2, tokens, HEAD_SIZE), bf16),
            pltpu.VMEM((2, tokens, HEAD_SIZE), bf16),
            pltpu.VMEM((2, 4, tokens, width), bf16),
            pltpu.VMEM((4, tokens, depth), f32),
            pltpu.VMEM((4, tokens, depth // 2), bf16),
            pltpu.VMEM((4, tokens, depth // 2), bf16),
            pltpu.VMEM((4, tokens, depth // 2), f32),
            pltpu.VMEM((4, tokens, depth // 2), bf16),
            pltpu.VMEM((4, tokens, depth // 2), bf16),
            pltpu.VMEM((tokens, depth), bf16),
            pltpu.VMEM((tokens, HEAD_SIZE), f32),
            pltpu.VMEM((tokens, HEAD_SIZE), f32),
            pltpu.VMEM((tokens, query_cols), bf16),
            dma((8,)),
            dma((4,)), dma((4,)), dma((4, 3)), dma((4, 3)), dma((2, 4)), dma((2, 2, 4)),
            dma((2,)), dma((2,)), dma((2,)), dma((2,)), dma((2, 4, 2)), dma((2, 4)),
            dma((4,)), dma((4,)), dma((4,)), dma((2,)), dma((4,)), dma((4,)),
        ],
        compiler_params=pltpu.CompilerParams(
            collective_id=0, has_side_effects=True, vmem_limit_bytes=60 * 1024 * 1024
        ),
    )(
        inputs, context_gradient, positions[None, :], frequency, sign, query_weight, key_value_weight.reshape(depth, -1),
    )
    return (grad_inputs, grad_query, grad_keyval.reshape(depth, 1, -1))


def on_device(inputs, context_gradient, positions, query_weight, key_value_weight):
    tok_rows = inputs.shape[0]
    block_rows = query_weight.shape[0]
    query_cols = query_weight.shape[1]
    local_heads = query_cols // HEAD_SIZE
    local_groups = key_value_weight.shape[2] // HEAD_SIZE
    sizes = tuple(lax.axis_size(axis) for axis in ("blk", "tp", "sub"))
    if sizes == (4, 2, 2) and (local_heads, local_groups) == (2 * QUERY_PER_GROUP, 4):
        return fused(inputs, context_gradient, positions, query_weight, key_value_weight)
    pair_index = lax.axis_index("sub")
    blocks = lax.axis_size("blk")
    sharers = lax.axis_size("tp") * lax.axis_size("sub")
    share = lax.axis_index("tp") * lax.axis_size("sub") + pair_index
    weight_cols = jnp.concatenate([query_weight, key_value_weight.reshape(block_rows, -1)], axis=1)
    share_rows = tok_rows // sharers
    shared = lax.dynamic_slice_in_dim(inputs, share * share_rows, share_rows, 0)
    shared = lax.all_to_all(
        shared.reshape(share_rows, blocks, block_rows).transpose(1, 0, 2), "blk", 0, 0, tiled=True
    )
    columns = lax.all_gather(shared, ("tp", "sub"), axis=1, tiled=True)

    def projection_term(block):
        rows = lax.dynamic_index_in_dim(columns, block, 0, keepdims=False)
        return jnp.dot(rows, weight_cols, preferred_element_type=jnp.float32)

    projection = ring_sum(projection_term, "blk")
    query_rows = projection[:, :query_cols].reshape(tok_rows, local_heads, HEAD_SIZE)
    own_proj = projection[:, query_cols:]
    peer_proj = from_partner(own_proj, "sub", 0)
    key_rows = jnp.where(pair_index == 0, own_proj, peer_proj).reshape(
        tok_rows, local_groups, HEAD_SIZE
    )
    value_rows = jnp.where(pair_index == 0, peer_proj, own_proj).reshape(
        tok_rows, local_groups, HEAD_SIZE
    )
    cosine_lookup, sine_lookup = rotary_tables(positions, HEAD_SIZE)
    query_rot = rotate(query_rows.astype(jnp.float32), cosine_lookup, sine_lookup).astype(
        jnp.bfloat16
    )
    key_rot = rotate(key_rows.astype(jnp.float32), cosine_lookup, sine_lookup).astype(jnp.bfloat16)
    head_group = (
        pair_index * local_heads + jnp.arange(local_heads, dtype=jnp.int32)
    ) // QUERY_PER_GROUP
    group_pick = (head_group[:, None] == jnp.arange(local_groups, dtype=jnp.int32)[None, :]).astype(
        jnp.bfloat16
    )
    key_full = jnp.einsum(
        "kgd,hg->khd", key_rot, group_pick, preferred_element_type=jnp.float32
    ).astype(jnp.bfloat16)
    value_full = jnp.einsum(
        "kgd,hg->khd", value_rows, group_pick, preferred_element_type=jnp.float32
    ).astype(jnp.bfloat16)
    grad_query, key_gradient, value_gradient = attend_back(
        query_rot,
        key_full,
        value_full,
        context_gradient.reshape(tok_rows, local_heads, HEAD_SIZE),
        allowed_pairs(positions),
    )
    query_gradient_rows = (
        inverse_rotation(grad_query, cosine_lookup, sine_lookup)
        .astype(jnp.bfloat16)
        .reshape(tok_rows, query_cols)
    )
    pick_float = group_pick.astype(jnp.float32)
    key_part = inverse_rotation(
        jnp.einsum("khd,hg->kgd", key_gradient, pick_float, precision=lax.Precision.HIGHEST),
        cosine_lookup,
        sine_lookup,
    )
    value_part = jnp.einsum(
        "khd,hg->kgd", value_gradient, pick_float, precision=lax.Precision.HIGHEST
    )
    mine = jnp.where(pair_index == 0, key_part, value_part)
    other = jnp.where(pair_index == 0, value_part, key_part)
    own_grads = (mine + from_partner(other, "sub", 0)).astype(jnp.bfloat16).reshape(tok_rows, -1)
    grad_proj = jnp.concatenate([query_gradient_rows, own_grads], axis=1)

    all_grads = ring_gather(grad_proj, "blk").reshape(blocks * tok_rows, -1)
    gradient_sum = lax.dot_general(
        columns.reshape(blocks * tok_rows, block_rows),
        all_grads,
        (((0,), (0,)), ((), ())),
        preferred_element_type=jnp.float32,
    ).astype(jnp.bfloat16)
    partial_inputs = lax.dot_general(
        all_grads, weight_cols, (((1,), (1,)), ((), ())), preferred_element_type=jnp.float32
    ).astype(jnp.bfloat16)
    pieces = lax.all_to_all(
        partial_inputs.reshape(sharers, -1, block_rows), ("tp", "sub"), 0, 0, tiled=True
    )
    grad_inputs = jnp.sum(pieces.astype(jnp.float32), axis=0).astype(jnp.bfloat16)
    swaps = [
        (b * sharers + s, s * sharers + b) for b in range(blocks) for s in range(sharers)
    ]
    grad_inputs = lax.ppermute(grad_inputs, ("blk", "tp", "sub"), swaps)
    grad_query_out = gradient_sum[:, :query_cols]
    grad_keyval_out = gradient_sum[:, query_cols:].reshape(block_rows, 1, -1)
    return (grad_inputs, grad_query_out, grad_keyval_out)


def solution(mesh):
    in_specs = (
        P(("parts", "blk"), None),
        P(("parts", "blk"), ("tp", "sub")),
        P(("parts", "blk")),
        P("blk", ("tp", "sub")),
        P("blk", "sub", "tp"),
    )
    out_specs = (
        P(("parts", "blk"), ("tp", "sub")),
        P(("parts", "blk"), ("tp", "sub")),
        P(("parts", "blk"), "sub", "tp"),
    )
    return jax.shard_map(
        on_device, mesh=mesh, in_specs=in_specs, out_specs=out_specs, check_vma=False
    )
```
